32 devices in a mesh: batch: 2 (over y), tm: 4 (over z), height: 4 (over x, core).
Axes of the slice: x: 2, y: 2, z: 4, core: 2. Of those that a mesh axis runs over, the one named last changes fastest.
Arguments:
- features: bfloat16 [2, 8, 32, 128, 128], P('batch', 'tm', 'height'), may hold values from -6 to 6
- w_spatial: bfloat16 [3, 3, 128, 128], replicated, may hold values from -0.1875 to 0.1875
- w_temporal: bfloat16 [3, 128, 128], replicated, may hold values from -0.3125 to 0.3125
- w_down: bfloat16 [3, 128, 128], replicated, may hold values from -0.3125 to 0.3125
- cotangent: bfloat16 [2, 4, 32, 128, 128], P('batch', 'tm', 'height'), may hold values from -40 to 40
Outputs:
- downsampled: bfloat16 [2, 4, 32, 128, 128], P('batch', 'tm', 'height')
- grad_features: bfloat16 [2, 8, 32, 128, 128], P('batch', 'tm', 'height')
- grad_spatial: float32 [3, 3, 128, 128], replicated
- grad_temporal: float32 [3, 128, 128], replicated
- grad_down: float32 [3, 128, 128], replicated
The draws below stay inside these ranges and needn't reach their ends.
All inputs are finite; a program needn't handle non-finite values.
Results may differ from the reference program's by a relative error of at most 0.0052.
Values may be sent and summed in bfloat16 or wider, within the bound.
A program may use at most 64 MiB of HBM per device.

```python
import jax
import jax.numpy as jnp

C = 128
WIDTH = 128
CLIPS = 2
FRAMES = 8
HEIGHT = 32


def draw_cotangent(key, part):
    key = jax.random.fold_in(key, 7)
    shape = (CLIPS, FRAMES // 2, HEIGHT, WIDTH, C)
    first = jax.random.fold_in(key, 0)
    third = jax.random.fold_in(key, 2)
    frame_pos = jnp.arange(FRAMES // 2, dtype=jnp.float32) / max(FRAMES // 2 - 1, 1)
    row_pos = jnp.arange(HEIGHT, dtype=jnp.float32) / max(HEIGHT - 1, 1)
    scale = jnp.exp(jnp.log(3.0) * frame_pos)[None, :, None, None, None] * jnp.exp(jnp.log(3.0) * row_pos)[None, None, :, None, None]
    chan = jnp.exp(jax.random.uniform(third, (C,), jnp.float32, 0.0, jnp.log(4.0)))
    values = jnp.clip(jax.random.normal(first, shape, jnp.float32), -4.0, 4.0) * scale * chan
    return jnp.clip(values, -40.0, 40.0).astype(jnp.bfloat16)


def shard_levels(rng, shape, cuts, least, top_value):
    level, own = 1.0, jax.random.fold_in(rng, 6)
    for dim, parts in cuts:
        draws = jnp.exp(jax.random.uniform(jax.random.fold_in(own, dim), (parts,), jnp.float32, least / len(cuts), top_value / len(cuts)))
        level = level * jnp.repeat(draws, shape[dim] // parts).reshape([-1 if axis == dim else 1 for axis in range(len(shape))])
    return level


def bell_draw(stream_key, dims, deviation, most, cuts=(), kind=jnp.bfloat16):
    drawn = jax.random.normal(stream_key, dims, jnp.float32) * deviation
    if len(cuts) > 0:
        drawn = shard_levels(stream_key, dims, cuts, -0.22, 0.18) * drawn
    return jnp.clip(drawn, min=-most, max=most).astype(kind)


def setup_inputs(seed: int = 0) -> dict:
    key_list = jax.random.split(jax.random.key(seed), 6)
    return {
        "features": bell_draw(key_list[0], (CLIPS, FRAMES, HEIGHT, WIDTH, C), 1.0, 6.0, ((0, 2), (1, 4), (2, 4))),
        "w_spatial": bell_draw(key_list[1], (3, 3, C, C), (9 * C) ** -0.5, 0.1875),
        "w_temporal": bell_draw(key_list[2], (3, C, C), (3 * C) ** -0.5, 0.3125),
        "w_down": bell_draw(key_list[3], (3, C, C), (3 * C) ** -0.5, 0.3125),
        "cotangent": draw_cotangent(jax.random.fold_in(key_list[5], 71), 0),
    }


def spatial(padded, kernel):
    rows = padded.shape[2] - 2
    cols = padded.shape[3]
    wide = jnp.pad(padded, ((0, 0), (0, 0), (0, 0), (1, 1), (0, 0))).astype(jnp.float32)
    kern = kernel.astype(jnp.float32)
    total = jnp.zeros(padded.shape[:2] + (rows, cols, kernel.shape[3]), jnp.float32)
    for dy in range(3):
        for dx in range(3):
            total = total + jnp.einsum('bfhwc,cd->bfhwd', wide[:, :, dy:dy + rows, dx:dx + cols], kern[dy, dx])
    return total

def spatial_grad(padded, grad):
    rows = grad.shape[2]
    cols = grad.shape[3]
    wide = jnp.pad(padded, ((0, 0), (0, 0), (0, 0), (1, 1), (0, 0))).astype(jnp.float32)
    gfl = grad.astype(jnp.float32)
    taps = []
    for dy in range(3):
        for dx in range(3):
            taps.append(jnp.einsum('bfhwc,bfhwd->cd', wide[:, :, dy:dy + rows, dx:dx + cols], gfl))
    return jnp.stack(taps).reshape(3, 3, grad.shape[4], grad.shape[4])

def temporal(padded, kernel):
    frames = padded.shape[1] - 2
    pfl = padded.astype(jnp.float32)
    kern = kernel.astype(jnp.float32)
    total = jnp.zeros(padded.shape[:1] + (frames,) + padded.shape[2:4] + (kernel.shape[2],), jnp.float32)
    for k in range(3):
        total = total + jnp.einsum('bfhwc,cd->bfhwd', pfl[:, k:k + frames], kern[k])
    return total

def reference(features, w_spatial, w_temporal, w_down, cotangent):
    frames = features.shape[1]
    half = frames // 2
    rowpad = ((0, 0), (0, 0), (1, 1), (0, 0), (0, 0))
    framepad = ((0, 0), (1, 1), (0, 0), (0, 0), (0, 0))
    xpad = jnp.pad(features, rowpad)
    pre = spatial(xpad, w_spatial)
    act = jax.nn.silu(pre).astype(jnp.bfloat16)
    act_pad = jnp.pad(act, framepad)
    mixed = temporal(act_pad, w_temporal)
    resid = (features.astype(jnp.float32) + mixed).astype(jnp.bfloat16)
    rpad = jnp.pad(resid, ((0, 0), (1, 0), (0, 0), (0, 0), (0, 0))).astype(jnp.float32)
    wd = w_down.astype(jnp.float32)
    gfl = cotangent.astype(jnp.float32)
    down = jnp.zeros(cotangent.shape, jnp.float32)
    grad_down = []
    for k in range(3):
        picked = rpad[:, k:k + 2 * half:2]
        down = down + jnp.einsum('bfhwc,cd->bfhwd', picked, wd[k])
        grad_down.append(jnp.einsum('bfhwc,bfhwd->cd', picked, gfl))
    grad_down = jnp.stack(grad_down)
    downsampled = down.astype(jnp.bfloat16)
    gnext = jnp.concatenate([gfl[:, 1:], jnp.zeros_like(gfl[:, :1])], axis=1)
    even = jnp.einsum('bfhwd,cd->bfhwc', gfl, wd[1])
    odd = jnp.einsum('bfhwd,cd->bfhwc', gfl, wd[2]) + jnp.einsum('bfhwd,cd->bfhwc', gnext, wd[0])
    g_resid = jnp.stack([even, odd], axis=2).reshape(features.shape)
    g_resid_b = g_resid.astype(jnp.bfloat16)
    flip_t = jnp.transpose(w_temporal[::-1], (0, 2, 1))
    g_act = temporal(jnp.pad(g_resid_b, framepad), flip_t)
    gr_fl = g_resid_b.astype(jnp.float32)
    apf = act_pad.astype(jnp.float32)
    grad_temporal = jnp.stack([jnp.einsum('bfhwc,bfhwd->cd', apf[:, k:k + frames], gr_fl) for k in range(3)])
    sig = jax.nn.sigmoid(pre)
    g_pre = (g_act * sig * (1.0 + pre * (1.0 - sig))).astype(jnp.bfloat16)
    grad_spatial = spatial_grad(xpad, g_pre)
    flip_s = jnp.transpose(w_spatial[::-1, ::-1], (0, 1, 3, 2))
    grad_features = (g_resid + spatial(jnp.pad(g_pre, rowpad), flip_s)).astype(jnp.bfloat16)
    return (downsampled, grad_features, grad_spatial, grad_temporal, grad_down)
```

```python
import functools

import jax
import jax.numpy as jnp
from jax import lax
from jax.experimental import pallas as pl
from jax.experimental.pallas import tpu as pltpu
from jax.sharding import PartitionSpec as P

MESH = pl.DeviceIdType.MESH
AXES = ("batch", "tm", "height")


def rows_each(mats, peers):
    return 16 * pl.cdiv(mats * 128, 16 * peers)


def sum_scratch(mats, peers, depth):
    rows = rows_each(mats, peers)
    return [
        pltpu.VMEM((peers * rows, 128), jnp.bfloat16),
        pltpu.VMEM((peers * rows, 128), jnp.bfloat16),
        pltpu.VMEM((depth * rows, 128), jnp.bfloat16),
        pltpu.VMEM((peers * rows, 128), jnp.bfloat16),
        pltpu.SemaphoreType.DMA((3, 2, max(peers, depth))),
    ]


class Sum:
    def __init__(self, dims, mats, refs):
        self.nb, self.nz, self.nh = dims
        self.mats = mats
        self.peers = self.nb * self.nh
        self.rows = rows_each(mats, self.peers)
        self.out, self.got, self.deep, self.full, self.sems = refs
        self.b, self.z, self.h = (lax.axis_index(a) for a in AXES)
        self.me = self.b * self.nh + self.h

    def slot(self, i):
        return pl.ds(pl.multiple_of(i * self.rows, 16), self.rows)

    def plane(self, o):
        p = lax.rem(self.me + o, self.peers)
        return p, (p // self.nh, self.z, lax.rem(p, self.nh))

    def scatter(self, o):
        p, dev = self.plane(o)
        return pltpu.make_async_remote_copy(
            src_ref=self.out.at[self.slot(p)],
            dst_ref=self.got.at[self.slot(self.me)],
            send_sem=self.sems.at[0, 0, o],
            recv_sem=self.sems.at[0, 1, o],
            device_id=dev,
            device_id_type=MESH,
        )

    def along(self, o):
        q = lax.rem(self.z + o, self.nz)
        return pltpu.make_async_remote_copy(
            src_ref=self.deep.at[self.slot(self.z)],
            dst_ref=self.deep.at[self.slot(self.z)],
            send_sem=self.sems.at[1, 0, o],
            recv_sem=self.sems.at[1, 1, o],
            device_id=(self.b, q, self.h),
            device_id_type=MESH,
        )

    def gather(self, o):
        _, dev = self.plane(o)
        return pltpu.make_async_remote_copy(
            src_ref=self.full.at[self.slot(self.me)],
            dst_ref=self.full.at[self.slot(self.me)],
            send_sem=self.sems.at[2, 0, o],
            recv_sem=self.sems.at[2, 1, o],
            device_id=dev,
            device_id_type=MESH,
        )

    def start(self):
        pad = self.peers * self.rows - self.mats * 128
        if pad:
            self.out[pl.ds(self.mats * 128, pad)] = jnp.zeros((pad, 128), jnp.bfloat16)
        for o in range(1, self.peers):
            self.scatter(o).start()

    def middle(self):
        total = self.out[self.slot(self.me)].astype(jnp.float32)
        for o in range(1, self.peers):
            self.scatter(o).wait()
            src = lax.rem(self.me - o + self.peers, self.peers)
            total = total + self.got[self.slot(src)].astype(jnp.float32)
        self.deep[self.slot(self.z)] = total.astype(jnp.bfloat16)
        for o in range(1, self.nz):
            self.along(o).start()

    def last(self):
        for o in range(1, self.nz):
            self.along(o).wait()
        total = self.deep[pl.ds(0, self.rows)].astype(jnp.float32)
        for q in range(1, self.nz):
            total = total + self.deep[pl.ds(q * self.rows, self.rows)].astype(jnp.float32)
        self.full[self.slot(self.me)] = total.astype(jnp.bfloat16)
        for o in range(1, self.peers):
            self.gather(o).start()

    def finish(self):
        for o in range(1, self.peers):
            self.gather(o).wait()


def greet(dims):
    nb, nz, nh = dims
    b, z, h = (lax.axis_index(a) for a in AXES)
    me = b * nh + h
    barrier = pltpu.get_barrier_semaphore()
    for o in range(1, nb * nh):
        p = lax.rem(me + o, nb * nh)
        pl.semaphore_signal(
            barrier, inc=1, device_id=(p // nh, z, lax.rem(p, nh)), device_id_type=MESH
        )
    for o in range(1, nz):
        pl.semaphore_signal(
            barrier, inc=1, device_id=(b, lax.rem(z + o, nz), h), device_id_type=MESH
        )
    pl.semaphore_wait(barrier, nb * nh - 1 + nz - 1)


def sum_kernel(dims, gs_ref, gt_ref, gd_ref, os_ref, ot_ref, od_ref, *refs):
    greet(dims)
    total = Sum(dims, 15, refs)
    for i in range(15):
        part = gs_ref[i // 3, i % 3] if i < 9 else gt_ref[i - 9] if i < 12 else gd_ref[i - 12]
        total.out[pl.ds(i * 128, 128)] = part.astype(jnp.bfloat16)
    total.start()
    total.middle()
    total.last()
    total.finish()
    for i in range(15):
        part = total.full[pl.ds(i * 128, 128)].astype(jnp.float32)
        if i < 9:
            os_ref[i // 3, i % 3] = part
        elif i < 12:
            ot_ref[i - 9] = part
        else:
            od_ref[i - 12] = part


def all_sum(gs, gt, gd):
    dims = tuple(lax.axis_size(a) for a in AXES)
    return pl.pallas_call(
        functools.partial(sum_kernel, dims),
        out_shape=[jax.ShapeDtypeStruct(g.shape, jnp.float32) for g in (gs, gt, gd)],
        in_specs=[pl.BlockSpec(memory_space=pltpu.VMEM)] * 3,
        out_specs=[pl.BlockSpec(memory_space=pltpu.VMEM)] * 3,
        scratch_shapes=sum_scratch(15, dims[0] * dims[2], dims[1]),
        compiler_params=pltpu.CompilerParams(
            collective_id=0, has_side_effects=True, vmem_limit_bytes=24 * 1024 * 1024
        ),
    )(gs, gt, gd)


def with_halo(block, sides, width):
    for axis, dim in sides:
        count = lax.axis_size(axis)
        forward = [(i, i + 1) for i in range(count - 1)]
        backward = [(target, source) for source, target in forward]
        low = lax.ppermute(
            lax.slice_in_dim(block, block.shape[dim] - width, None, axis=dim), axis, forward
        )
        high = lax.ppermute(lax.slice_in_dim(block, 0, width, axis=dim), axis, backward)
        block = jnp.concatenate([low, block, high], axis=dim)
    return block


def from_behind(shard, axis, by):
    count = lax.axis_size(axis)
    pairs = [(i, i + by) for i in range(count) if 0 <= i + by < count]
    return lax.ppermute(shard, axis, pairs)


def spatial(padded, kernel):
    rows = padded.shape[2] - 2
    cols = padded.shape[3]
    wide = jnp.pad(padded, ((0, 0), (0, 0), (0, 0), (1, 1), (0, 0)))
    total = jnp.zeros(padded.shape[:2] + (rows, cols, kernel.shape[3]), jnp.float32)
    for dy in range(3):
        for dx in range(3):
            total = total + jnp.einsum(
                "bfhwc,cd->bfhwd",
                wide[:, :, dy : dy + rows, dx : dx + cols],
                kernel[dy, dx],
                preferred_element_type=jnp.float32,
            )
    return total


def spatial_grad(padded, grad):
    rows = grad.shape[2]
    cols = grad.shape[3]
    wide = jnp.pad(padded, ((0, 0), (0, 0), (0, 0), (1, 1), (0, 0)))
    taps = []
    for dy in range(3):
        for dx in range(3):
            taps.append(
                jnp.einsum(
                    "bfhwc,bfhwd->cd",
                    wide[:, :, dy : dy + rows, dx : dx + cols],
                    grad,
                    preferred_element_type=jnp.float32,
                )
            )
    return jnp.stack(taps).reshape(3, 3, grad.shape[4], grad.shape[4])


def temporal(padded, kernel):
    frames = padded.shape[1] - 2
    total = jnp.zeros(
        padded.shape[:1] + (frames,) + padded.shape[2:4] + (kernel.shape[2],), jnp.float32
    )
    for k in range(3):
        total = total + jnp.einsum(
            "bfhwc,cd->bfhwd",
            padded[:, k : k + frames],
            kernel[k],
            preferred_element_type=jnp.float32,
        )
    return total


def per_device(features, w_spatial, w_temporal, w_down, cotangent):
    frames = features.shape[1]
    half = cotangent.shape[1]
    xpad = with_halo(features, (("height", 2),), 1)
    pre = spatial(xpad, w_spatial)
    act = jax.nn.silu(pre).astype(jnp.bfloat16)
    act_pad = with_halo(act, (("tm", 1),), 1)
    mixed = temporal(act_pad, w_temporal)
    resid = (features.astype(jnp.float32) + mixed).astype(jnp.bfloat16)
    before = from_behind(resid[:, -1:], "tm", 1)
    rpad = jnp.concatenate([before, resid], axis=1)
    down = jnp.zeros(cotangent.shape, jnp.float32)
    grad_down = []
    for k in range(3):
        picked = rpad[:, k : k + 2 * half : 2]
        down = down + jnp.einsum(
            "bfhwc,cd->bfhwd", picked, w_down[k], preferred_element_type=jnp.float32
        )
        grad_down.append(
            jnp.einsum("bfhwc,bfhwd->cd", picked, cotangent, preferred_element_type=jnp.float32)
        )
    grad_down = jnp.stack(grad_down)
    downsampled = down.astype(jnp.bfloat16)
    after = from_behind(cotangent, "tm", -1)
    gnext = jnp.concatenate([cotangent[:, 1:], after], axis=1)
    even = jnp.einsum("bfhwd,cd->bfhwc", cotangent, w_down[1], preferred_element_type=jnp.float32)
    odd = jnp.einsum("bfhwd,cd->bfhwc", cotangent, w_down[2], preferred_element_type=jnp.float32)
    odd = odd + jnp.einsum("bfhwd,cd->bfhwc", gnext, w_down[0], preferred_element_type=jnp.float32)
    g_resid = jnp.stack([even, odd], axis=2).reshape(features.shape)
    g_resid_b = g_resid.astype(jnp.bfloat16)
    gpad = with_halo(g_resid_b, (("tm", 1),), 1)
    flip_t = jnp.transpose(w_temporal[::-1], (0, 2, 1))
    g_act = temporal(gpad, flip_t)
    grad_temporal = jnp.stack(
        [
            jnp.einsum(
                "bfhwc,bfhwd->cd",
                act_pad[:, k : k + frames],
                g_resid_b,
                preferred_element_type=jnp.float32,
            )
            for k in range(3)
        ]
    )
    sig = jax.nn.sigmoid(pre)
    g_pre = (g_act * sig * (1.0 + pre * (1.0 - sig))).astype(jnp.bfloat16)
    grad_spatial = spatial_grad(xpad, g_pre)
    g_prepad = with_halo(g_pre, (("height", 2),), 1)
    flip_s = jnp.transpose(w_spatial[::-1, ::-1], (0, 1, 3, 2))
    grad_features = (g_resid + spatial(g_prepad, flip_s)).astype(jnp.bfloat16)
    grad_spatial, grad_temporal, grad_down = all_sum(grad_spatial, grad_temporal, grad_down)
    return (downsampled, grad_features, grad_spatial, grad_temporal, grad_down)


def solution(mesh):
    placed = (
        P("batch", "tm", "height", None, None),
        P(),
        P(),
        P(),
        P("batch", "tm", "height", None, None),
    )
    return jax.shard_map(
        per_device,
        mesh=mesh,
        in_specs=placed,
        out_specs=(
            P("batch", "tm", "height", None, None),
            P("batch", "tm", "height", None, None),
            P(),
            P(),
            P(),
        ),
        check_vma=False,
    )
```

```python
import functools

import jax
import jax.numpy as jnp
from jax import lax
from jax.experimental import pallas as pl
from jax.experimental.pallas import tpu as pltpu
from jax.sharding import PartitionSpec as P

MESH = pl.DeviceIdType.MESH
AXES = ("batch", "tm", "height")


def rows_each(mats, peers):
    return 16 * pl.cdiv(mats * 128, 16 * peers)


def sum_scratch(mats, peers, depth):
    rows = rows_each(mats, peers)
    return [
        pltpu.VMEM((peers * rows, 128), jnp.bfloat16),
        pltpu.VMEM((peers * rows, 128), jnp.bfloat16),
        pltpu.VMEM((depth * rows, 128), jnp.bfloat16),
        pltpu.VMEM((peers * rows, 128), jnp.bfloat16),
        pltpu.SemaphoreType.DMA((3, 2, max(peers, depth))),
    ]


class Sum:
    def __init__(self, dims, mats, refs):
        self.nb, self.nz, self.nh = dims
        self.mats = mats
        self.peers = self.nb * self.nh
        self.rows = rows_each(mats, self.peers)
        self.out, self.got, self.deep, self.full, self.sems = refs
        self.b, self.z, self.h = (lax.axis_index(a) for a in AXES)
        self.me = self.b * self.nh + self.h

    def slot(self, i):
        return pl.ds(pl.multiple_of(i * self.rows, 16), self.rows)

    def plane(self, o):
        p = lax.rem(self.me + o, self.peers)
        return p, (p // self.nh, self.z, lax.rem(p, self.nh))

    def scatter(self, o):
        p, dev = self.plane(o)
        return pltpu.make_async_remote_copy(
            src_ref=self.out.at[self.slot(p)],
            dst_ref=self.got.at[self.slot(self.me)],
            send_sem=self.sems.at[0, 0, o],
            recv_sem=self.sems.at[0, 1, o],
            device_id=dev,
            device_id_type=MESH,
        )

    def along(self, o):
        q = lax.rem(self.z + o, self.nz)
        return pltpu.make_async_remote_copy(
            src_ref=self.deep.at[self.slot(self.z)],
            dst_ref=self.deep.at[self.slot(self.z)],
            send_sem=self.sems.at[1, 0, o],
            recv_sem=self.sems.at[1, 1, o],
            device_id=(self.b, q, self.h),
            device_id_type=MESH,
        )

    def gather(self, o):
        _, dev = self.plane(o)
        return pltpu.make_async_remote_copy(
            src_ref=self.full.at[self.slot(self.me)],
            dst_ref=self.full.at[self.slot(self.me)],
            send_sem=self.sems.at[2, 0, o],
            recv_sem=self.sems.at[2, 1, o],
            device_id=dev,
            device_id_type=MESH,
        )

    def start(self):
        pad = self.peers * self.rows - self.mats * 128
        if pad:
            self.out[pl.ds(self.mats * 128, pad)] = jnp.zeros((pad, 128), jnp.bfloat16)
        for o in range(1, self.peers):
            self.scatter(o).start()

    def middle(self):
        total = self.out[self.slot(self.me)].astype(jnp.float32)
        for o in range(1, self.peers):
            self.scatter(o).wait()
            src = lax.rem(self.me - o + self.peers, self.peers)
            total = total + self.got[self.slot(src)].astype(jnp.float32)
        self.deep[self.slot(self.z)] = total.astype(jnp.bfloat16)
        for o in range(1, self.nz):
            self.along(o).start()

    def last(self):
        for o in range(1, self.nz):
            self.along(o).wait()
        total = self.deep[pl.ds(0, self.rows)].astype(jnp.float32)
        for q in range(1, self.nz):
            total = total + self.deep[pl.ds(q * self.rows, self.rows)].astype(jnp.float32)
        self.full[self.slot(self.me)] = total.astype(jnp.bfloat16)
        for o in range(1, self.peers):
            self.gather(o).start()

    def finish(self):
        for o in range(1, self.peers):
            self.gather(o).wait()


def greet(dims):
    nb, nz, nh = dims
    b, z, h = (lax.axis_index(a) for a in AXES)
    me = b * nh + h
    barrier = pltpu.get_barrier_semaphore()
    for o in range(1, nb * nh):
        p = lax.rem(me + o, nb * nh)
        pl.semaphore_signal(
            barrier, inc=1, device_id=(p // nh, z, lax.rem(p, nh)), device_id_type=MESH
        )
    for o in range(1, nz):
        pl.semaphore_signal(
            barrier, inc=1, device_id=(b, lax.rem(z + o, nz), h), device_id_type=MESH
        )
    pl.semaphore_wait(barrier, nb * nh - 1 + nz - 1)


class Edge:
    def __init__(self, src, dst, sems, axis, step):
        size, at = lax.axis_size(axis), lax.axis_index(axis)
        self.sends = at < size - 1 if step > 0 else at > 0
        self.gets = at > 0 if step > 0 else at < size - 1
        self.copy = pltpu.make_async_remote_copy(
            src_ref=src,
            dst_ref=dst,
            send_sem=sems.at[0],
            recv_sem=sems.at[1],
            device_id=tuple(lax.axis_index(a) + (step if a == axis else 0) for a in AXES),
            device_id_type=MESH,
        )
        self.dst = dst

    def start(self):
        @pl.when(self.sends)
        def _():
            self.copy.start()

        @pl.when(jnp.logical_not(self.gets))
        def _():
            self.dst[...] = jnp.zeros(self.dst.shape, self.dst.dtype)

    def arrive(self):
        @pl.when(self.gets)
        def _():
            self.copy.wait_recv()

    def leave(self):
        @pl.when(self.sends)
        def _():
            self.copy.wait_send()


def dot(a, b):
    return jnp.dot(a, b, preferred_element_type=jnp.float32)


def from_left(v, col):
    return jnp.where(col == 0, 0.0, pltpu.roll(v, 1, 0))


def from_right(v, col, width):
    return jnp.where(col == width - 1, 0.0, pltpu.roll(v, v.shape[0] - 1, 0))


def kernel(
    dims, step, x_ref, ws_ref, wt_ref, wd_ref, c_ref,
    down_ref, gx_ref, os_ref, ot_ref, od_ref,
    xp, xt, gp, gcat, act, slope, gres, gb, cm, cp, lcat, part, d_out, e_out, d_in, e_in,
    wf, wb, tcat, tflip, dflip, dback, edge_sems, *sums,
):
    _, rows, width, ch = x_ref.shape[1:]
    tokens = rows * width
    per = step * width
    half = len(sums) // 2
    big, small = Sum(dims, 9, sums[:half]), Sum(dims, 6, sums[half:])
    edges = [
        Edge(x_ref.at[0, :, rows - 1], xp.at[:, 0], edge_sems.at[0], "height", 1),
        Edge(x_ref.at[0, :, 0], xp.at[:, rows + 1], edge_sems.at[1], "height", -1),
        Edge(c_ref.at[0, 0], cm, edge_sems.at[2], "tm", 1),
        Edge(c_ref.at[0, 0], cp, edge_sems.at[3], "tm", -1),
        Edge(gp.at[:, rows], gp.at[:, 0], edge_sems.at[4], "height", 1),
        Edge(gp.at[:, 1], gp.at[:, rows + 1], edge_sems.at[5], "height", -1),
        Edge(d_out, d_in, edge_sems.at[6], "tm", 1),
        Edge(e_out, e_in, edge_sems.at[7], "tm", -1),
    ]
    inner = (lax.axis_index("tm") > 0).astype(jnp.float32)
    col = lax.broadcasted_iota(jnp.int32, (step, width, ch), 1).reshape(per, ch)

    greet(dims)
    for e in edges[:4]:
        e.start()
    for f in range(2):
        xp[f, pl.ds(1, rows)] = x_ref[0, f]
    for k in range(3):
        tcat[:, (2 - k) * ch : (3 - k) * ch] = wt_ref[k]
        tflip[k * ch : (k + 1) * ch, :] = wt_ref[k].T
        dflip[:, k * ch : (k + 1) * ch] = wd_ref[k].T
        for dx in range(3):
            w = ws_ref[k, dx]
            wf[k * ch : (k + 1) * ch, dx * ch : (dx + 1) * ch] = w
            wb[(2 - k) * ch : (3 - k) * ch, (2 - dx) * ch : (3 - dx) * ch] = w.T
    dback[0:ch, :] = dflip[:, 2 * ch : 3 * ch]
    dback[ch : 2 * ch, :] = dflip[:, 0:ch]

    def flat(v):
        return v.reshape(per, ch)

    def tall(v):
        return v.reshape(step, width, ch)

    def conv(ref, f, y, weights):
        wide = jnp.concatenate([flat(ref[f, pl.ds(y + dy, step)]) for dy in range(3)], axis=1)
        out = dot(wide, weights[...])
        return (
            out[:, ch : 2 * ch]
            + from_left(out[:, :ch], col)
            + from_right(out[:, 2 * ch :], col, width)
        )

    for e in edges[:2]:
        e.arrive()
    cuts = rows // step

    def forward(i, carry):
        f, y = i // cuts, (i % cuts) * step
        pre = conv(xp, f, y, wf)
        sig = jax.nn.sigmoid(pre)
        act[f, pl.ds(y, step)] = tall((pre * sig).astype(jnp.bfloat16))
        slope[f, pl.ds(y, step)] = tall(sig * (1.0 + pre * (1.0 - sig)))
        return carry

    lax.fori_loop(0, 2 * cuts, forward, 0)

    for f in range(2):
        xt[f] = xp[f].reshape((rows + 2) * width, ch).T

    for e in edges[2:4]:
        e.arrive()

    def backward(i, carry):
        at = pl.ds(i * step, step)
        c0, before, after = flat(c_ref[0, 0, at]), flat(cm[at]), flat(cp[at])
        g0 = dot(jnp.concatenate([before, c0], axis=1), dback[...]) * inner
        mid = dot(c0, dflip[:, ch:])
        far = dot(after, dflip[:, : 2 * ch])
        g1, g2, g3 = mid[:, :ch], mid[:, ch:] + far[:, :ch], far[:, ch:]
        gres[0, at] = tall(g1)
        gres[1, at] = tall(g2)
        g = [v.astype(jnp.bfloat16) for v in (g0, g1, g2, g3)]
        for n in range(4):
            gb[n, at] = tall(g[n])
        for a in range(2):
            wide = jnp.concatenate([g[a + 2], g[a + 1], g[a]], axis=1)
            gpre = dot(wide, tflip[...]) * flat(slope[a, at])
            low = gpre.astype(jnp.bfloat16)
            gp[a, pl.ds(i * step + 1, step)] = tall(low)
            gcat[a, at, :, :ch] = tall(from_right(gpre, col, width).astype(jnp.bfloat16))
            gcat[a, at, :, ch : 2 * ch] = tall(low)
            gcat[a, at, :, 2 * ch :] = tall(from_left(gpre, col).astype(jnp.bfloat16))
        return carry

    lax.fori_loop(0, cuts, backward, 0)
    for e in edges[4:6]:
        e.start()

    total = jnp.zeros((3 * ch, 3 * ch), jnp.float32)
    for f in range(2):
        left = jnp.concatenate(
            [xt[f, :, dy * width : dy * width + tokens] for dy in range(3)], axis=0
        )
        total = total + dot(left, gcat[f].reshape(tokens, 3 * ch))
    for dy in range(3):
        for dx in range(3):
            big.out[pl.ds((dy * 3 + dx) * ch, ch)] = total[
                dy * ch : (dy + 1) * ch, dx * ch : (dx + 1) * ch
            ].astype(jnp.bfloat16)
    big.start()

    def mixing(i, carry):
        at = pl.ds(i * step, step)
        y0 = dot(flat(act[0, at]), tcat[...])
        y1 = dot(flat(act[1, at]), tcat[...])
        x0 = flat(x_ref[0, 0, at]).astype(jnp.float32)
        x1 = flat(x_ref[0, 1, at]).astype(jnp.float32)
        l0 = (y0[:, :ch] * inner).astype(jnp.bfloat16)
        l1 = (x0 + y0[:, ch : 2 * ch] + y1[:, :ch]).astype(jnp.bfloat16)
        l2 = (x1 + y0[:, 2 * ch :] + y1[:, ch : 2 * ch]).astype(jnp.bfloat16)
        u = y1[:, 2 * ch :].astype(jnp.bfloat16)
        for n, v in enumerate((l0, l1, l2, u)):
            lcat[n, at] = tall(v)
        own = jnp.concatenate([l0, l1, l2], axis=1)
        part[at] = tall(dot(own, wd_ref[...].reshape(3 * ch, ch)))
        ahead = jnp.concatenate([l2, u], axis=1)
        d_out[at] = tall(dot(ahead, wd_ref[0:2].reshape(2 * ch, ch)).astype(jnp.bfloat16))
        e_out[at] = tall(dot(l0, wd_ref[2]).astype(jnp.bfloat16))
        return carry

    lax.fori_loop(0, cuts, mixing, 0)
    for e in edges[6:]:
        e.start()

    times = jnp.zeros((ch, 3 * ch), jnp.float32)
    for a in range(2):
        wide = jnp.concatenate([gb[n].reshape(tokens, ch) for n in (a + 2, a + 1, a)], axis=1)
        times = times + dot(act[a].reshape(tokens, ch).T, wide)
    left = jnp.concatenate([lcat[n].reshape(tokens, ch).T for n in range(4)], axis=0)
    wide = jnp.concatenate([v.reshape(tokens, ch) for v in (cp[...], c_ref[0, 0], cm[...])], axis=1)
    outer = dot(left, wide)

    def block(n, m):
        return outer[n * ch : (n + 1) * ch, m * ch : (m + 1) * ch]

    downs = (block(2, 0) + block(0, 1), block(1, 1) + block(3, 0), block(2, 1) + block(0, 2))
    for k in range(3):
        small.out[pl.ds(k * ch, ch)] = times[:, k * ch : (k + 1) * ch].astype(jnp.bfloat16)
        small.out[pl.ds((3 + k) * ch, ch)] = downs[k].astype(jnp.bfloat16)
    small.start()

    big.middle()
    for e in edges[4:6]:
        e.arrive()

    def features(f):
        def body(i, carry):
            at = pl.ds(i * step, step)
            out = conv(gp, f, i * step, wb) + flat(gres[f, at])
            gx_ref[0, f, at] = tall(out.astype(jnp.bfloat16))
            return carry

        lax.fori_loop(0, cuts, body, 0)

    features(0)
    small.middle()
    big.last()
    features(1)
    small.last()
    for e in edges[6:]:
        e.arrive()
    down_ref[0, 0] = (
        part[...] + d_in[...].astype(jnp.float32) + e_in[...].astype(jnp.float32)
    ).astype(jnp.bfloat16)
    big.finish()
    for i in range(9):
        os_ref[i // 3, i % 3] = big.full[pl.ds(i * ch, ch)].astype(jnp.float32)
    small.finish()
    for i in range(3):
        ot_ref[i] = small.full[pl.ds(i * ch, ch)].astype(jnp.float32)
        od_ref[i] = small.full[pl.ds((3 + i) * ch, ch)].astype(jnp.float32)
    for e in edges:
        e.leave()


def per_device(features, w_spatial, w_temporal, w_down, cotangent):
    dims = tuple(lax.axis_size(a) for a in AXES)
    _, frames, rows, width, ch = features.shape
    peers = dims[0] * dims[2]
    step = 4
    bf, f32 = jnp.bfloat16, jnp.float32
    frame = (rows, width, ch)
    return pl.pallas_call(
        functools.partial(kernel, dims, step),
        out_shape=[
            jax.ShapeDtypeStruct(cotangent.shape, bf),
            jax.ShapeDtypeStruct(features.shape, bf),
            jax.ShapeDtypeStruct(w_spatial.shape, f32),
            jax.ShapeDtypeStruct(w_temporal.shape, f32),
            jax.ShapeDtypeStruct(w_down.shape, f32),
        ],
        in_specs=[pl.BlockSpec(memory_space=pltpu.VMEM)] * 5,
        out_specs=[pl.BlockSpec(memory_space=pltpu.VMEM)] * 5,
        scratch_shapes=[
            pltpu.VMEM((2, rows + 2, width, ch), bf),
            pltpu.VMEM((2, ch, (rows + 2) * width), bf),
            pltpu.VMEM((2, rows + 2, width, ch), bf),
            pltpu.VMEM((2, rows, width, 3 * ch), bf),
            pltpu.VMEM((2,) + frame, bf),
            pltpu.VMEM((2,) + frame, f32),
            pltpu.VMEM((2,) + frame, f32),
            pltpu.VMEM((4,) + frame, bf),
            pltpu.VMEM(frame, bf),
            pltpu.VMEM(frame, bf),
            pltpu.VMEM((4,) + frame, bf),
            pltpu.VMEM(frame, f32),
            pltpu.VMEM(frame, bf),
            pltpu.VMEM(frame, bf),
            pltpu.VMEM(frame, bf),
            pltpu.VMEM(frame, bf),
            pltpu.VMEM((3 * ch, 3 * ch), bf),
            pltpu.VMEM((3 * ch, 3 * ch), bf),
            pltpu.VMEM((ch, 3 * ch), bf),
            pltpu.VMEM((3 * ch, ch), bf),
            pltpu.VMEM((ch, 3 * ch), bf),
            pltpu.VMEM((2 * ch, ch), bf),
            pltpu.SemaphoreType.DMA((8, 2)),
        ]
        + sum_scratch(9, peers, dims[1])
        + sum_scratch(6, peers, dims[1]),
        compiler_params=pltpu.CompilerParams(
            collective_id=0, has_side_effects=True, vmem_limit_bytes=40 * 1024 * 1024
        ),
    )(features, w_spatial, w_temporal, w_down, cotangent)


def solution(mesh):
    placed = (
        P("batch", "tm", "height", None, None),
        P(),
        P(),
        P(),
        P("batch", "tm", "height", None, None),
    )
    return jax.shard_map(
        per_device,
        mesh=mesh,
        in_specs=placed,
        out_specs=(
            P("batch", "tm", "height", None, None),
            P("batch", "tm", "height", None, None),
            P(),
            P(),
            P(),
        ),
        check_vma=False,
    )
```

```python
import functools

import jax
import jax.numpy as jnp
from jax import lax
from jax.experimental import pallas as pl
from jax.experimental.pallas import tpu as pltpu
from jax.sharding import PartitionSpec as P

MESH = pl.DeviceIdType.MESH
AXES = ("batch", "tm", "height")


def rows_each(mats, peers):
    return 16 * pl.cdiv(mats * 128, 16 * peers)


def sum_scratch(mats, peers, depth):
    rows = rows_each(mats, peers)
    return [
        pltpu.VMEM((peers * rows, 128), jnp.bfloat16),
        pltpu.VMEM((peers * rows, 128), jnp.bfloat16),
        pltpu.VMEM((depth * rows, 128), jnp.bfloat16),
        pltpu.VMEM((peers * rows, 128), jnp.bfloat16),
        pltpu.SemaphoreType.DMA((3, 2, max(peers, depth))),
    ]


class Sum:
    def __init__(self, dims, mats, refs):
        self.nb, self.nz, self.nh = dims
        self.mats = mats
        self.peers = self.nb * self.nh
        self.rows = rows_each(mats, self.peers)
        self.out, self.got, self.deep, self.full, self.sems = refs
        self.b, self.z, self.h = (lax.axis_index(a) for a in AXES)
        self.me = self.b * self.nh + self.h

    def slot(self, i):
        return pl.ds(pl.multiple_of(i * self.rows, 16), self.rows)

    def plane(self, o):
        p = lax.rem(self.me + o, self.peers)
        return p, (p // self.nh, self.z, lax.rem(p, self.nh))

    def scatter(self, o):
        p, dev = self.plane(o)
        return pltpu.make_async_remote_copy(
            src_ref=self.out.at[self.slot(p)],
            dst_ref=self.got.at[self.slot(self.me)],
            send_sem=self.sems.at[0, 0, o],
            recv_sem=self.sems.at[0, 1, o],
            device_id=dev,
            device_id_type=MESH,
        )

    def along(self, o):
        q = lax.rem(self.z + o, self.nz)
        return pltpu.make_async_remote_copy(
            src_ref=self.deep.at[self.slot(self.z)],
            dst_ref=self.deep.at[self.slot(self.z)],
            send_sem=self.sems.at[1, 0, o],
            recv_sem=self.sems.at[1, 1, o],
            device_id=(self.b, q, self.h),
            device_id_type=MESH,
        )

    def gather(self, o):
        _, dev = self.plane(o)
        return pltpu.make_async_remote_copy(
            src_ref=self.full.at[self.slot(self.me)],
            dst_ref=self.full.at[self.slot(self.me)],
            send_sem=self.sems.at[2, 0, o],
            recv_sem=self.sems.at[2, 1, o],
            device_id=dev,
            device_id_type=MESH,
        )

    def start(self):
        pad = self.peers * self.rows - self.mats * 128
        if pad:
            self.out[pl.ds(self.mats * 128, pad)] = jnp.zeros((pad, 128), jnp.bfloat16)
        for o in range(1, self.peers):
            self.scatter(o).start()

    def middle(self):
        total = self.out[self.slot(self.me)].astype(jnp.float32)
        for o in range(1, self.peers):
            self.scatter(o).wait()
            src = lax.rem(self.me - o + self.peers, self.peers)
            total = total + self.got[self.slot(src)].astype(jnp.float32)
        self.deep[self.slot(self.z)] = total.astype(jnp.bfloat16)
        for o in range(1, self.nz):
            self.along(o).start()

    def last(self):
        for o in range(1, self.nz):
            self.along(o).wait()
        total = self.deep[pl.ds(0, self.rows)].astype(jnp.float32)
        for q in range(1, self.nz):
            total = total + self.deep[pl.ds(q * self.rows, self.rows)].astype(jnp.float32)
        self.full[self.slot(self.me)] = total.astype(jnp.bfloat16)
        for o in range(1, self.peers):
            self.gather(o).start()

    def finish(self):
        for o in range(1, self.peers):
            self.gather(o).wait()


def greet(dims):
    nb, nz, nh = dims
    b, z, h = (lax.axis_index(a) for a in AXES)
    me = b * nh + h
    barrier = pltpu.get_barrier_semaphore()
    for o in range(1, nb * nh):
        p = lax.rem(me + o, nb * nh)
        pl.semaphore_signal(
            barrier, inc=1, device_id=(p // nh, z, lax.rem(p, nh)), device_id_type=MESH
        )
    for o in range(1, nz):
        pl.semaphore_signal(
            barrier, inc=1, device_id=(b, lax.rem(z + o, nz), h), device_id_type=MESH
        )
    pl.semaphore_wait(barrier, nb * nh - 1 + nz - 1)


class Edge:
    def __init__(self, src, dst, sems, axis, step):
        size, at = lax.axis_size(axis), lax.axis_index(axis)
        self.sends = at < size - 1 if step > 0 else at > 0
        self.gets = at > 0 if step > 0 else at < size - 1
        self.copy = pltpu.make_async_remote_copy(
            src_ref=src,
            dst_ref=dst,
            send_sem=sems.at[0],
            recv_sem=sems.at[1],
            device_id=tuple(lax.axis_index(a) + (step if a == axis else 0) for a in AXES),
            device_id_type=MESH,
        )
        self.dst = dst

    def start(self):
        @pl.when(self.sends)
        def _():
            self.copy.start()

        @pl.when(jnp.logical_not(self.gets))
        def _():
            self.dst[...] = jnp.zeros(self.dst.shape, self.dst.dtype)

    def arrive(self):
        @pl.when(self.gets)
        def _():
            self.copy.wait_recv()

    def leave(self):
        @pl.when(self.sends)
        def _():
            self.copy.wait_send()


def dot(a, b):
    return jnp.dot(a, b, preferred_element_type=jnp.float32)


def from_left(v, col):
    return jnp.where(col == 0, 0.0, pltpu.roll(v, 1, 0))


def from_right(v, col, width):
    return jnp.where(col == width - 1, 0.0, pltpu.roll(v, v.shape[0] - 1, 0))


def kernel(
    dims, step, x_hbm, ws_hbm, wt_hbm, wd_hbm, c_hbm,
    down_ref, gx_ref, os_ref, ot_ref, od_ref,
    xp, xt, gp, gcat, act, slope, gres, gb, cm, cp, lcat, part, d_out, e_out, d_in, e_in,
    ws_ref, wt_ref, wd_ref, c_ref, wf, wb, tcat, tflip, dflip, dback, load_sems, edge_sems, *sums,
):
    _, rows, width, ch = x_hbm.shape[1:]
    cuts = rows // step
    tokens = rows * width
    per = step * width
    half = len(sums) // 2
    big, small = Sum(dims, 9, sums[:half]), Sum(dims, 6, sums[half:])
    edges = [
        Edge(x_hbm.at[0, :, rows - 1], xp.at[:, 0], edge_sems.at[0], "height", 1),
        Edge(x_hbm.at[0, :, 0], xp.at[:, rows + 1], edge_sems.at[1], "height", -1),
        Edge(gp.at[:, rows], gp.at[:, 0], edge_sems.at[2], "height", 1),
        Edge(gp.at[:, 1], gp.at[:, rows + 1], edge_sems.at[3], "height", -1),
        Edge(d_out, d_in, edge_sems.at[4], "tm", 1),
        Edge(e_out, e_in, edge_sems.at[5], "tm", -1),
    ]
    near = []
    for i in range(cuts):
        at = pl.ds(i * step, step)
        near.append(
            (
                Edge(c_hbm.at[0, 0, at], cm.at[at], edge_sems.at[6 + 2 * i], "tm", 1),
                Edge(c_hbm.at[0, 0, at], cp.at[at], edge_sems.at[7 + 2 * i], "tm", -1),
            )
        )
    loads = [
        pltpu.make_async_copy(src, dst, load_sems.at[i])
        for i, (src, dst) in enumerate(
            (
                (ws_hbm, ws_ref),
                (x_hbm.at[0], xp.at[:, pl.ds(1, rows)]),
                (wt_hbm, wt_ref),
                (wd_hbm, wd_ref),
                (c_hbm, c_ref),
            )
        )
    ]
    inner = (lax.axis_index("tm") > 0).astype(jnp.float32)
    col = lax.broadcasted_iota(jnp.int32, (step, width, ch), 1).reshape(per, ch)

    for copy in loads:
        copy.start()
    greet(dims)
    for e in edges[:2]:
        e.start()
    for pair in near:
        for e in pair:
            e.start()
    for copy in loads:
        copy.wait()
    for k in range(3):
        tcat[:, (2 - k) * ch : (3 - k) * ch] = wt_ref[k]
        tflip[k * ch : (k + 1) * ch, :] = wt_ref[k].T
        dflip[:, k * ch : (k + 1) * ch] = wd_ref[k].T
        for dx in range(3):
            w = ws_ref[k, dx]
            wf[k * ch : (k + 1) * ch, dx * ch : (dx + 1) * ch] = w
            wb[(2 - k) * ch : (3 - k) * ch, (2 - dx) * ch : (3 - dx) * ch] = w.T
    dback[0:ch, :] = dflip[:, 2 * ch : 3 * ch]
    dback[ch : 2 * ch, :] = dflip[:, 0:ch]

    def flat(v):
        return v.reshape(per, ch)

    def tall(v):
        return v.reshape(step, width, ch)

    def conv(ref, f, y, weights):
        wide = jnp.concatenate([flat(ref[f, pl.ds(y + dy, step)]) for dy in range(3)], axis=1)
        out = dot(wide, weights[...])
        return (
            out[:, ch : 2 * ch]
            + from_left(out[:, :ch], col)
            + from_right(out[:, 2 * ch :], col, width)
        )

    for f in range(2):
        xt[f, :, width : (rows + 1) * width] = xp[f, pl.ds(1, rows)].reshape(tokens, ch).T
    for e in edges[:2]:
        e.arrive()

    def forward(i, carry):
        f, y = i // cuts, (i % cuts) * step
        pre = conv(xp, f, y, wf)
        sig = jax.nn.sigmoid(pre)
        act[f, pl.ds(y, step)] = tall((pre * sig).astype(jnp.bfloat16))
        slope[f, pl.ds(y, step)] = tall(sig * (1.0 + pre * (1.0 - sig)))
        return carry

    lax.fori_loop(0, 2 * cuts, forward, 0)

    for f in range(2):
        xt[f, :, :width] = xp[f, 0].T
        xt[f, :, (rows + 1) * width :] = xp[f, rows + 1].T

    def mixing(i, carry):
        at = pl.ds(i * step, step)
        y0 = dot(flat(act[0, at]), tcat[...])
        y1 = dot(flat(act[1, at]), tcat[...])
        x0 = flat(xp[0, pl.ds(i * step + 1, step)]).astype(jnp.float32)
        x1 = flat(xp[1, pl.ds(i * step + 1, step)]).astype(jnp.float32)
        l0 = (y0[:, :ch] * inner).astype(jnp.bfloat16)
        l1 = (x0 + y0[:, ch : 2 * ch] + y1[:, :ch]).astype(jnp.bfloat16)
        l2 = (x1 + y0[:, 2 * ch :] + y1[:, ch : 2 * ch]).astype(jnp.bfloat16)
        u = y1[:, 2 * ch :].astype(jnp.bfloat16)
        for n, v in enumerate((l0, l1, l2, u)):
            lcat[n, at] = tall(v)
        own = jnp.concatenate([l0, l1, l2], axis=1)
        part[at] = tall(dot(own, wd_ref[...].reshape(3 * ch, ch)))
        ahead = jnp.concatenate([l2, u], axis=1)
        d_out[at] = tall(dot(ahead, wd_ref[0:2].reshape(2 * ch, ch)).astype(jnp.bfloat16))
        e_out[at] = tall(dot(l0, wd_ref[2]).astype(jnp.bfloat16))
        return carry

    lax.fori_loop(0, cuts, mixing, 0)
    for e in edges[4:]:
        e.start()

    def backward(i):
        at = pl.ds(i * step, step)
        c0, before, after = flat(c_ref[0, 0, at]), flat(cm[at]), flat(cp[at])
        g0 = dot(jnp.concatenate([before, c0], axis=1), dback[...]) * inner
        mid = dot(c0, dflip[:, ch:])
        far = dot(after, dflip[:, : 2 * ch])
        g1, g2, g3 = mid[:, :ch], mid[:, ch:] + far[:, :ch], far[:, ch:]
        gres[0, at] = tall(g1)
        gres[1, at] = tall(g2)
        g = [v.astype(jnp.bfloat16) for v in (g0, g1, g2, g3)]
        for n in range(4):
            gb[n, at] = tall(g[n])
        for a in range(2):
            wide = jnp.concatenate([g[a + 2], g[a + 1], g[a]], axis=1)
            gpre = dot(wide, tflip[...]) * flat(slope[a, at])
            low = gpre.astype(jnp.bfloat16)
            gp[a, pl.ds(i * step + 1, step)] = tall(low)
            gcat[a, at, :, :ch] = tall(from_right(gpre, col, width).astype(jnp.bfloat16))
            gcat[a, at, :, ch : 2 * ch] = tall(low)
            gcat[a, at, :, 2 * ch :] = tall(from_left(gpre, col).astype(jnp.bfloat16))

    for i in range(cuts):
        for e in near[i]:
            e.arrive()
        backward(i)
    for e in edges[2:4]:
        e.start()

    total = jnp.zeros((3 * ch, 3 * ch), jnp.float32)
    for f in range(2):
        left = jnp.concatenate(
            [xt[f, :, dy * width : dy * width + tokens] for dy in range(3)], axis=0
        )
        total = total + dot(left, gcat[f].reshape(tokens, 3 * ch))
    for dy in range(3):
        for dx in range(3):
            big.out[pl.ds((dy * 3 + dx) * ch, ch)] = total[
                dy * ch : (dy + 1) * ch, dx * ch : (dx + 1) * ch
            ].astype(jnp.bfloat16)
    big.start()

    times = jnp.zeros((ch, 3 * ch), jnp.float32)
    for a in range(2):
        wide = jnp.concatenate([gb[n].reshape(tokens, ch) for n in (a + 2, a + 1, a)], axis=1)
        times = times + dot(act[a].reshape(tokens, ch).T, wide)
    left = jnp.concatenate([lcat[n].reshape(tokens, ch).T for n in range(4)], axis=0)
    wide = jnp.concatenate([v.reshape(tokens, ch) for v in (cp[...], c_ref[0, 0], cm[...])], axis=1)
    outer = dot(left, wide)

    def block(n, m):
        return outer[n * ch : (n + 1) * ch, m * ch : (m + 1) * ch]

    downs = (block(2, 0) + block(0, 1), block(1, 1) + block(3, 0), block(2, 1) + block(0, 2))
    for k in range(3):
        small.out[pl.ds(k * ch, ch)] = times[:, k * ch : (k + 1) * ch].astype(jnp.bfloat16)
        small.out[pl.ds((3 + k) * ch, ch)] = downs[k].astype(jnp.bfloat16)
    small.start()

    big.middle()
    for e in edges[2:4]:
        e.arrive()

    def features(f):
        def body(i, carry):
            at = pl.ds(i * step, step)
            out = conv(gp, f, i * step, wb) + flat(gres[f, at])
            gx_ref[0, f, at] = tall(out.astype(jnp.bfloat16))
            return carry

        lax.fori_loop(0, cuts, body, 0)

    features(0)
    small.middle()
    big.last()
    features(1)
    small.last()
    for e in edges[4:]:
        e.arrive()
    down_ref[0, 0] = (
        part[...] + d_in[...].astype(jnp.float32) + e_in[...].astype(jnp.float32)
    ).astype(jnp.bfloat16)
    big.finish()
    for i in range(9):
        os_ref[i // 3, i % 3] = big.full[pl.ds(i * ch, ch)].astype(jnp.float32)
    small.finish()
    for i in range(3):
        ot_ref[i] = small.full[pl.ds(i * ch, ch)].astype(jnp.float32)
        od_ref[i] = small.full[pl.ds((3 + i) * ch, ch)].astype(jnp.float32)
    for e in edges:
        e.leave()
    for pair in near:
        for e in pair:
            e.leave()


def store(*refs):
    sems = refs[-1]
    copies = [pltpu.make_async_copy(refs[i], refs[5 + i], sems.at[i]) for i in range(5)]
    for copy in copies:
        copy.start()
    for copy in copies:
        copy.wait()


def per_device(features, w_spatial, w_temporal, w_down, cotangent):
    args = (features, w_spatial, w_temporal, w_down, cotangent)
    dims = tuple(lax.axis_size(a) for a in AXES)
    _, frames, rows, width, ch = features.shape
    peers = dims[0] * dims[2]
    step = 4
    bf, f32 = jnp.bfloat16, jnp.float32
    frame = (rows, width, ch)
    shapes = [
        jax.ShapeDtypeStruct(cotangent.shape, bf),
        jax.ShapeDtypeStruct(features.shape, bf),
        jax.ShapeDtypeStruct(w_spatial.shape, f32),
        jax.ShapeDtypeStruct(w_temporal.shape, f32),
        jax.ShapeDtypeStruct(w_down.shape, f32),
    ]
    outs = pl.pallas_call(
        functools.partial(kernel, dims, step),
        out_shape=shapes,
        in_specs=[pl.BlockSpec(memory_space=pltpu.HBM)] * 5,
        out_specs=[pl.BlockSpec(memory_space=pltpu.VMEM)] * 5,
        scratch_shapes=[
            pltpu.VMEM((2, rows + 2, width, ch), bf),
            pltpu.VMEM((2, ch, (rows + 2) * width), bf),
            pltpu.VMEM((2, rows + 2, width, ch), bf),
            pltpu.VMEM((2, rows, width, 3 * ch), bf),
            pltpu.VMEM((2,) + frame, bf),
            pltpu.VMEM((2,) + frame, f32),
            pltpu.VMEM((2,) + frame, f32),
            pltpu.VMEM((4,) + frame, bf),
            pltpu.VMEM(frame, bf),
            pltpu.VMEM(frame, bf),
            pltpu.VMEM((4,) + frame, bf),
            pltpu.VMEM(frame, f32),
            pltpu.VMEM(frame, bf),
            pltpu.VMEM(frame, bf),
            pltpu.VMEM(frame, bf),
            pltpu.VMEM(frame, bf),
            pltpu.VMEM(w_spatial.shape, bf),
            pltpu.VMEM(w_temporal.shape, bf),
            pltpu.VMEM(w_down.shape, bf),
            pltpu.VMEM(cotangent.shape, bf),
            pltpu.VMEM((3 * ch, 3 * ch), bf),
            pltpu.VMEM((3 * ch, 3 * ch), bf),
            pltpu.VMEM((ch, 3 * ch), bf),
            pltpu.VMEM((3 * ch, ch), bf),
            pltpu.VMEM((ch, 3 * ch), bf),
            pltpu.VMEM((2 * ch, ch), bf),
            pltpu.SemaphoreType.DMA((5,)),
            pltpu.SemaphoreType.DMA((6 + 2 * rows // step, 2)),
        ]
        + sum_scratch(9, peers, dims[1])
        + sum_scratch(6, peers, dims[1]),
        compiler_params=pltpu.CompilerParams(
            collective_id=0, has_side_effects=True, vmem_limit_bytes=40 * 1024 * 1024
        ),
    )(*(pltpu.with_memory_space_constraint(v, pltpu.HBM) for v in args))
    return pl.pallas_call(
        store,
        out_shape=shapes,
        in_specs=[pl.BlockSpec(memory_space=pltpu.VMEM)] * 5,
        out_specs=[pl.BlockSpec(memory_space=pltpu.HBM)] * 5,
        scratch_shapes=[pltpu.SemaphoreType.DMA((5,))],
    )(*outs)


def solution(mesh):
    placed = (
        P("batch", "tm", "height", None, None),
        P(),
        P(),
        P(),
        P("batch", "tm", "height", None, None),
    )
    return jax.shard_map(
        per_device,
        mesh=mesh,
        in_specs=placed,
        out_specs=(
            P("batch", "tm", "height", None, None),
            P("batch", "tm", "height", None, None),
            P(),
            P(),
            P(),
        ),
        check_vma=False,
    )
```

```python
import functools

import jax
import jax.numpy as jnp
from jax import lax
from jax.experimental import pallas as pl
from jax.experimental.pallas import tpu as pltpu
from jax.sharding import PartitionSpec as P

MESH = pl.DeviceIdType.MESH
AXES = ("batch", "tm", "height")


def rows_each(mats, peers):
    return 16 * pl.cdiv(mats * 128, 16 * peers)


def sum_scratch(mats, peers, depth):
    rows = rows_each(mats, peers)
    half = peers // 2 * rows
    return [
        pltpu.VMEM((2 * half, 128), jnp.float32),
        pltpu.VMEM((half, 128), jnp.bfloat16),
        pltpu.VMEM((half, 128), jnp.bfloat16),
        pltpu.VMEM((half, 128), jnp.bfloat16),
        pltpu.VMEM((half, 128), jnp.bfloat16),
        pltpu.VMEM((depth * rows, 128), jnp.bfloat16),
        pltpu.VMEM((2 * half, 128), jnp.bfloat16),
        pltpu.SemaphoreType.DMA((5, 2, max(peers // 2, depth))),
    ]


class Sum:
    def __init__(self, dims, mats, refs):
        self.nb, self.nz, self.nh = dims
        self.mats = mats
        self.rows = rows_each(mats, self.nb * self.nh)
        self.out, self.give, self.take, self.send, self.got, self.deep, self.full, self.sems = refs
        self.b, self.z, self.h = (lax.axis_index(a) for a in AXES)
        self.wide = self.nh // 2
        self.chips = self.nb * self.wide
        self.core = lax.rem(self.h, 2)
        self.me = self.b * self.wide + self.h // 2

    def slot(self, i):
        return pl.ds(pl.multiple_of(i * self.rows, 16), self.rows)

    def half(self, core):
        size = self.chips * self.rows
        return pl.ds(pl.multiple_of(core * size, 16), size)

    def copy(self, src, dst, stage, n, dev):
        return pltpu.make_async_remote_copy(
            src_ref=src,
            dst_ref=dst,
            send_sem=self.sems.at[stage, 0, n],
            recv_sem=self.sems.at[stage, 1, n],
            device_id=dev,
            device_id_type=MESH,
        )

    def partner(self):
        return (self.b, self.z, self.h + 1 - 2 * self.core)

    def chip(self, o):
        p = lax.rem(self.me + o, self.chips)
        return p, (p // self.wide, self.z, lax.rem(p, self.wide) * 2 + self.core)

    def behind(self, o):
        return lax.rem(self.me - o + self.chips, self.chips)

    def swap(self):
        return self.copy(self.give, self.take, 0, 0, self.partner())

    def scatter(self, o):
        p, dev = self.chip(o)
        return self.copy(self.send.at[self.slot(p)], self.got.at[self.slot(self.me)], 1, o, dev)

    def along(self, o):
        q = lax.rem(self.z + o, self.nz)
        mine = self.deep.at[self.slot(self.z)]
        return self.copy(mine, mine, 2, o, (self.b, q, self.h))

    def gather(self, o):
        _, dev = self.chip(o)
        mine = self.full.at[self.slot(self.core * self.chips + self.me)]
        return self.copy(mine, mine, 3, o, dev)

    def forward(self, o):
        piece = self.full.at[self.slot(self.core * self.chips + self.behind(o))]
        return self.copy(piece, piece, 4, o, self.partner())

    def pair(self):
        pad = 2 * self.chips * self.rows - self.mats * 128
        if pad:
            self.out[pl.ds(self.mats * 128, pad)] = jnp.zeros((pad, 128), jnp.float32)
        self.give[...] = self.out[self.half(1 - self.core)].astype(jnp.bfloat16)
        self.swap().start()

    def start(self):
        self.swap().wait()
        total = self.out[self.half(self.core)] + self.take[...].astype(jnp.float32)
        self.send[...] = total.astype(jnp.bfloat16)
        for o in range(1, self.chips):
            self.scatter(o).start()

    def middle(self):
        total = self.send[self.slot(self.me)].astype(jnp.float32)
        for o in range(1, self.chips):
            self.scatter(o).wait()
            total = total + self.got[self.slot(self.behind(o))].astype(jnp.float32)
        self.deep[self.slot(self.z)] = total.astype(jnp.bfloat16)
        for o in range(1, self.nz):
            self.along(o).start()

    def last(self):
        for o in range(1, self.nz):
            self.along(o).wait()
        total = self.deep[pl.ds(0, self.rows)].astype(jnp.float32)
        for q in range(1, self.nz):
            total = total + self.deep[pl.ds(q * self.rows, self.rows)].astype(jnp.float32)
        mine = self.slot(self.core * self.chips + self.me)
        self.full[mine] = total.astype(jnp.bfloat16)
        for o in range(1, self.chips):
            self.gather(o).start()
        self.forward(0).start()

    def finish(self):
        for o in range(1, self.chips):
            self.gather(o).wait()
            self.forward(o).start()
        for o in range(self.chips):
            self.forward(o).wait()


def greet(dims):
    nb, nz, nh = dims
    b, z, h = (lax.axis_index(a) for a in AXES)
    me = b * nh + h
    barrier = pltpu.get_barrier_semaphore()
    for o in range(1, nb * nh):
        p = lax.rem(me + o, nb * nh)
        pl.semaphore_signal(
            barrier, inc=1, device_id=(p // nh, z, lax.rem(p, nh)), device_id_type=MESH
        )
    for o in range(1, nz):
        pl.semaphore_signal(
            barrier, inc=1, device_id=(b, lax.rem(z + o, nz), h), device_id_type=MESH
        )
    pl.semaphore_wait(barrier, nb * nh - 1 + nz - 1)


class Edge:
    def __init__(self, src, dst, sems, axis, step):
        size, at = lax.axis_size(axis), lax.axis_index(axis)
        self.sends = at < size - 1 if step > 0 else at > 0
        self.gets = at > 0 if step > 0 else at < size - 1
        self.copy = pltpu.make_async_remote_copy(
            src_ref=src,
            dst_ref=dst,
            send_sem=sems.at[0],
            recv_sem=sems.at[1],
            device_id=tuple(lax.axis_index(a) + (step if a == axis else 0) for a in AXES),
            device_id_type=MESH,
        )
        self.dst = dst

    def start(self):
        @pl.when(self.sends)
        def _():
            self.copy.start()

        @pl.when(jnp.logical_not(self.gets))
        def _():
            self.dst[...] = jnp.zeros(self.dst.shape, self.dst.dtype)

    def arrive(self):
        @pl.when(self.gets)
        def _():
            self.copy.wait_recv()

    def leave(self):
        @pl.when(self.sends)
        def _():
            self.copy.wait_send()


def dot(a, b):
    return jnp.dot(a, b, preferred_element_type=jnp.float32)


def from_left(v, col):
    return jnp.where(col == 0, 0.0, pltpu.roll(v, 1, 0))


def from_right(v, col, width):
    return jnp.where(col == width - 1, 0.0, pltpu.roll(v, v.shape[0] - 1, 0))


def kernel(
    dims, step, x_hbm, ws_hbm, wt_hbm, wd_hbm, c_hbm,
    down_ref, gx_ref, os_ref, ot_ref, od_ref,
    xp, xt, gp, gcat, act, slope, gres, gb, cm, cp, lcat, part, d_out, e_out, d_in, e_in,
    ws_ref, wt_ref, wd_ref, c_ref, wf, wb, tcat, tflip, dflip, dback, load_sems, edge_sems, *sums,
):
    _, rows, width, ch = x_hbm.shape[1:]
    cuts = rows // step
    tokens = rows * width
    per = step * width
    half = len(sums) // 2
    big, small = Sum(dims, 9, sums[:half]), Sum(dims, 6, sums[half:])
    edges = [
        Edge(x_hbm.at[0, :, rows - 1], xp.at[:, 0], edge_sems.at[0], "height", 1),
        Edge(x_hbm.at[0, :, 0], xp.at[:, rows + 1], edge_sems.at[1], "height", -1),
        Edge(gp.at[:, rows], gp.at[:, 0], edge_sems.at[2], "height", 1),
        Edge(gp.at[:, 1], gp.at[:, rows + 1], edge_sems.at[3], "height", -1),
        Edge(d_out, d_in, edge_sems.at[4], "tm", 1),
        Edge(e_out, e_in, edge_sems.at[5], "tm", -1),
    ]
    near = []
    for i in range(cuts):
        at = pl.ds(i * step, step)
        near.append(
            (
                Edge(c_hbm.at[0, 0, at], cm.at[at], edge_sems.at[6 + 2 * i], "tm", 1),
                Edge(c_hbm.at[0, 0, at], cp.at[at], edge_sems.at[7 + 2 * i], "tm", -1),
            )
        )
    loads = [
        pltpu.make_async_copy(src, dst, load_sems.at[i])
        for i, (src, dst) in enumerate(
            (
                (ws_hbm, ws_ref),
                (x_hbm.at[0], xp.at[:, pl.ds(1, rows)]),
                (wt_hbm, wt_ref),
                (wd_hbm, wd_ref),
                (c_hbm, c_ref),
            )
        )
    ]
    inner = (lax.axis_index("tm") > 0).astype(jnp.float32)
    col = lax.broadcasted_iota(jnp.int32, (step, width, ch), 1).reshape(per, ch)

    for copy in loads:
        copy.start()
    greet(dims)
    for e in edges[:2]:
        e.start()
    for pair in near:
        for e in pair:
            e.start()
    for copy in loads:
        copy.wait()
    for k in range(3):
        tcat[:, (2 - k) * ch : (3 - k) * ch] = wt_ref[k]
        tflip[k * ch : (k + 1) * ch, :] = wt_ref[k].T
        dflip[:, k * ch : (k + 1) * ch] = wd_ref[k].T
        for dx in range(3):
            w = ws_ref[k, dx]
            wf[k * ch : (k + 1) * ch, dx * ch : (dx + 1) * ch] = w
            wb[(2 - k) * ch : (3 - k) * ch, (2 - dx) * ch : (3 - dx) * ch] = w.T
    dback[0:ch, :] = dflip[:, 2 * ch : 3 * ch]
    dback[ch : 2 * ch, :] = dflip[:, 0:ch]

    def flat(v):
        return v.reshape(per, ch)

    def tall(v):
        return v.reshape(step, width, ch)

    def conv(ref, f, y, weights):
        wide = jnp.concatenate([flat(ref[f, pl.ds(y + dy, step)]) for dy in range(3)], axis=1)
        out = dot(wide, weights[...])
        return (
            out[:, ch : 2 * ch]
            + from_left(out[:, :ch], col)
            + from_right(out[:, 2 * ch :], col, width)
        )

    for f in range(2):
        xt[f, :, width : (rows + 1) * width] = xp[f, pl.ds(1, rows)].reshape(tokens, ch).T
    for e in edges[:2]:
        e.arrive()

    def forward(i, carry):
        f, y = i // cuts, (i % cuts) * step
        pre = conv(xp, f, y, wf)
        sig = jax.nn.sigmoid(pre)
        act[f, pl.ds(y, step)] = tall((pre * sig).astype(jnp.bfloat16))
        slope[f, pl.ds(y, step)] = tall(sig * (1.0 + pre * (1.0 - sig)))
        return carry

    lax.fori_loop(0, 2 * cuts, forward, 0)

    for f in range(2):
        xt[f, :, :width] = xp[f, 0].T
        xt[f, :, (rows + 1) * width :] = xp[f, rows + 1].T

    def mixing(i, carry):
        at = pl.ds(i * step, step)
        y0 = dot(flat(act[0, at]), tcat[...])
        y1 = dot(flat(act[1, at]), tcat[...])
        x0 = flat(xp[0, pl.ds(i * step + 1, step)]).astype(jnp.float32)
        x1 = flat(xp[1, pl.ds(i * step + 1, step)]).astype(jnp.float32)
        l0 = (y0[:, :ch] * inner).astype(jnp.bfloat16)
        l1 = (x0 + y0[:, ch : 2 * ch] + y1[:, :ch]).astype(jnp.bfloat16)
        l2 = (x1 + y0[:, 2 * ch :] + y1[:, ch : 2 * ch]).astype(jnp.bfloat16)
        u = y1[:, 2 * ch :].astype(jnp.bfloat16)
        for n, v in enumerate((l0, l1, l2, u)):
            lcat[n, at] = tall(v)
        own = jnp.concatenate([l0, l1, l2], axis=1)
        part[at] = tall(dot(own, wd_ref[...].reshape(3 * ch, ch)))
        ahead = jnp.concatenate([l2, u], axis=1)
        d_out[at] = tall(dot(ahead, wd_ref[0:2].reshape(2 * ch, ch)).astype(jnp.bfloat16))
        e_out[at] = tall(dot(l0, wd_ref[2]).astype(jnp.bfloat16))
        return carry

    lax.fori_loop(0, cuts, mixing, 0)
    for e in edges[4:]:
        e.start()

    def backward(i):
        at = pl.ds(i * step, step)
        c0, before, after = flat(c_ref[0, 0, at]), flat(cm[at]), flat(cp[at])
        g0 = dot(jnp.concatenate([before, c0], axis=1), dback[...]) * inner
        mid = dot(c0, dflip[:, ch:])
        far = dot(after, dflip[:, : 2 * ch])
        g1, g2, g3 = mid[:, :ch], mid[:, ch:] + far[:, :ch], far[:, ch:]
        gres[0, at] = tall(g1)
        gres[1, at] = tall(g2)
        g = [v.astype(jnp.bfloat16) for v in (g0, g1, g2, g3)]
        for n in range(4):
            gb[n, at] = tall(g[n])
        for a in range(2):
            wide = jnp.concatenate([g[a + 2], g[a + 1], g[a]], axis=1)
            gpre = dot(wide, tflip[...]) * flat(slope[a, at])
            low = gpre.astype(jnp.bfloat16)
            gp[a, pl.ds(i * step + 1, step)] = tall(low)
            gcat[a, at, :, :ch] = tall(from_right(gpre, col, width).astype(jnp.bfloat16))
            gcat[a, at, :, ch : 2 * ch] = tall(low)
            gcat[a, at, :, 2 * ch :] = tall(from_left(gpre, col).astype(jnp.bfloat16))

    for i in range(cuts):
        for e in near[i]:
            e.arrive()
        backward(i)
    for e in edges[2:4]:
        e.start()

    total = jnp.zeros((3 * ch, 3 * ch), jnp.float32)
    for f in range(2):
        left = jnp.concatenate(
            [xt[f, :, dy * width : dy * width + tokens] for dy in range(3)], axis=0
        )
        total = total + dot(left, gcat[f].reshape(tokens, 3 * ch))
    for dy in range(3):
        for dx in range(3):
            big.out[pl.ds((dy * 3 + dx) * ch, ch)] = total[
                dy * ch : (dy + 1) * ch, dx * ch : (dx + 1) * ch
            ]
    big.pair()

    times = jnp.zeros((ch, 3 * ch), jnp.float32)
    for a in range(2):
        wide = jnp.concatenate([gb[n].reshape(tokens, ch) for n in (a + 2, a + 1, a)], axis=1)
        times = times + dot(act[a].reshape(tokens, ch).T, wide)
    big.start()
    left = jnp.concatenate([lcat[n].reshape(tokens, ch).T for n in range(4)], axis=0)
    wide = jnp.concatenate([v.reshape(tokens, ch) for v in (cp[...], c_ref[0, 0], cm[...])], axis=1)
    outer = dot(left, wide)

    def block(n, m):
        return outer[n * ch : (n + 1) * ch, m * ch : (m + 1) * ch]

    downs = (block(2, 0) + block(0, 1), block(1, 1) + block(3, 0), block(2, 1) + block(0, 2))
    for k in range(3):
        small.out[pl.ds(k * ch, ch)] = times[:, k * ch : (k + 1) * ch]
        small.out[pl.ds((3 + k) * ch, ch)] = downs[k]
    small.pair()
    for e in edges[2:4]:
        e.arrive()

    def features(f):
        def body(i, carry):
            at = pl.ds(i * step, step)
            out = conv(gp, f, i * step, wb) + flat(gres[f, at])
            gx_ref[0, f, at] = tall(out.astype(jnp.bfloat16))
            return carry

        lax.fori_loop(0, cuts, body, 0)

    features(0)
    small.start()
    big.middle()
    features(1)
    small.middle()
    big.last()
    for e in edges[4:]:
        e.arrive()
    down_ref[0, 0] = (
        part[...] + d_in[...].astype(jnp.float32) + e_in[...].astype(jnp.float32)
    ).astype(jnp.bfloat16)
    small.last()
    big.finish()
    for i in range(9):
        os_ref[i // 3, i % 3] = big.full[pl.ds(i * ch, ch)].astype(jnp.float32)
    small.finish()
    for i in range(3):
        ot_ref[i] = small.full[pl.ds(i * ch, ch)].astype(jnp.float32)
        od_ref[i] = small.full[pl.ds((3 + i) * ch, ch)].astype(jnp.float32)
    for e in edges:
        e.leave()
    for pair in near:
        for e in pair:
            e.leave()


def store(*refs):
    sems = refs[-1]
    copies = [pltpu.make_async_copy(refs[i], refs[5 + i], sems.at[i]) for i in range(5)]
    for copy in copies:
        copy.start()
    for copy in copies:
        copy.wait()


def per_device(features, w_spatial, w_temporal, w_down, cotangent):
    args = (features, w_spatial, w_temporal, w_down, cotangent)
    dims = tuple(lax.axis_size(a) for a in AXES)
    _, frames, rows, width, ch = features.shape
    peers = dims[0] * dims[2]
    step = 4
    bf, f32 = jnp.bfloat16, jnp.float32
    frame = (rows, width, ch)
    shapes = [
        jax.ShapeDtypeStruct(cotangent.shape, bf),
        jax.ShapeDtypeStruct(features.shape, bf),
        jax.ShapeDtypeStruct(w_spatial.shape, f32),
        jax.ShapeDtypeStruct(w_temporal.shape, f32),
        jax.ShapeDtypeStruct(w_down.shape, f32),
    ]
    outs = pl.pallas_call(
        functools.partial(kernel, dims, step),
        out_shape=shapes,
        in_specs=[pl.BlockSpec(memory_space=pltpu.HBM)] * 5,
        out_specs=[pl.BlockSpec(memory_space=pltpu.VMEM)] * 5,
        scratch_shapes=[
            pltpu.VMEM((2, rows + 2, width, ch), bf),
            pltpu.VMEM((2, ch, (rows + 2) * width), bf),
            pltpu.VMEM((2, rows + 2, width, ch), bf),
            pltpu.VMEM((2, rows, width, 3 * ch), bf),
            pltpu.VMEM((2,) + frame, bf),
            pltpu.VMEM((2,) + frame, f32),
            pltpu.VMEM((2,) + frame, f32),
            pltpu.VMEM((4,) + frame, bf),
            pltpu.VMEM(frame, bf),
            pltpu.VMEM(frame, bf),
            pltpu.VMEM((4,) + frame, bf),
            pltpu.VMEM(frame, f32),
            pltpu.VMEM(frame, bf),
            pltpu.VMEM(frame, bf),
            pltpu.VMEM(frame, bf),
            pltpu.VMEM(frame, bf),
            pltpu.VMEM(w_spatial.shape, bf),
            pltpu.VMEM(w_temporal.shape, bf),
            pltpu.VMEM(w_down.shape, bf),
            pltpu.VMEM(cotangent.shape, bf),
            pltpu.VMEM((3 * ch, 3 * ch), bf),
            pltpu.VMEM((3 * ch, 3 * ch), bf),
            pltpu.VMEM((ch, 3 * ch), bf),
            pltpu.VMEM((3 * ch, ch), bf),
            pltpu.VMEM((ch, 3 * ch), bf),
            pltpu.VMEM((2 * ch, ch), bf),
            pltpu.SemaphoreType.DMA((5,)),
            pltpu.SemaphoreType.DMA((6 + 2 * rows // step, 2)),
        ]
        + sum_scratch(9, peers, dims[1])
        + sum_scratch(6, peers, dims[1]),
        compiler_params=pltpu.CompilerParams(
            collective_id=0, has_side_effects=True, vmem_limit_bytes=40 * 1024 * 1024
        ),
    )(*(pltpu.with_memory_space_constraint(v, pltpu.HBM) for v in args))
    return pl.pallas_call(
        store,
        out_shape=shapes,
        in_specs=[pl.BlockSpec(memory_space=pltpu.VMEM)] * 5,
        out_specs=[pl.BlockSpec(memory_space=pltpu.HBM)] * 5,
        scratch_shapes=[pltpu.SemaphoreType.DMA((5,))],
        compiler_params=pltpu.CompilerParams(vmem_limit_bytes=4 * 1024 * 1024),
    )(*outs)


def solution(mesh):
    placed = (
        P("batch", "tm", "height", None, None),
        P(),
        P(),
        P(),
        P("batch", "tm", "height", None, None),
    )
    return jax.shard_map(
        per_device,
        mesh=mesh,
        in_specs=placed,
        out_specs=(
            P("batch", "tm", "height", None, None),
            P("batch", "tm", "height", None, None),
            P(),
            P(),
            P(),
        ),
        check_vma=False,
    )
```

```python
import functools

import jax
import jax.numpy as jnp
from jax import lax
from jax.experimental import pallas as pl
from jax.experimental.pallas import tpu as pltpu
from jax.sharding import PartitionSpec as P

MESH = pl.DeviceIdType.MESH
AXES = ("batch", "tm", "height")


def rows_each(mats, peers):
    return 16 * pl.cdiv(mats * 128, 16 * peers)


def sum_scratch(mats, peers, depth):
    rows = rows_each(mats, peers)
    half = peers // 2 * rows
    return [
        pltpu.VMEM((2 * half, 128), jnp.float32),
        pltpu.VMEM((half, 128), jnp.bfloat16),
        pltpu.VMEM((half, 128), jnp.bfloat16),
        pltpu.VMEM((half, 128), jnp.bfloat16),
        pltpu.VMEM((half, 128), jnp.bfloat16),
        pltpu.VMEM((depth * rows, 128), jnp.bfloat16),
        pltpu.VMEM((2 * half, 128), jnp.bfloat16),
        pltpu.SemaphoreType.DMA((5, 2, max(peers // 2, depth))),
    ]


class Sum:
    def __init__(self, dims, mats, refs):
        self.nb, self.nz, self.nh = dims
        self.mats = mats
        self.rows = rows_each(mats, self.nb * self.nh)
        self.out, self.give, self.take, self.send, self.got, self.deep, self.full, self.sems = refs
        self.b, self.z, self.h = (lax.axis_index(a) for a in AXES)
        self.wide = self.nh // 2
        self.chips = self.nb * self.wide
        self.core = lax.rem(self.h, 2)
        self.me = self.b * self.wide + self.h // 2

    def slot(self, i):
        return pl.ds(pl.multiple_of(i * self.rows, 16), self.rows)

    def half(self, core):
        size = self.chips * self.rows
        return pl.ds(pl.multiple_of(core * size, 16), size)

    def copy(self, src, dst, stage, n, dev):
        return pltpu.make_async_remote_copy(
            src_ref=src,
            dst_ref=dst,
            send_sem=self.sems.at[stage, 0, n],
            recv_sem=self.sems.at[stage, 1, n],
            device_id=dev,
            device_id_type=MESH,
        )

    def partner(self):
        return (self.b, self.z, self.h + 1 - 2 * self.core)

    def chip(self, o):
        p = lax.rem(self.me + o, self.chips)
        return p, (p // self.wide, self.z, lax.rem(p, self.wide) * 2 + self.core)

    def behind(self, o):
        return lax.rem(self.me - o + self.chips, self.chips)

    def swap(self):
        return self.copy(self.give, self.take, 0, 0, self.partner())

    def scatter(self, o):
        p, dev = self.chip(o)
        return self.copy(self.send.at[self.slot(p)], self.got.at[self.slot(self.me)], 1, o, dev)

    def along(self, o):
        q = lax.rem(self.z + o, self.nz)
        mine = self.deep.at[self.slot(self.z)]
        return self.copy(mine, mine, 2, o, (self.b, q, self.h))

    def gather(self, o):
        _, dev = self.chip(o)
        mine = self.full.at[self.slot(self.core * self.chips + self.me)]
        return self.copy(mine, mine, 3, o, dev)

    def forward(self, o):
        piece = self.full.at[self.slot(self.core * self.chips + self.behind(o))]
        return self.copy(piece, piece, 4, o, self.partner())

    def pair(self):
        pad = 2 * self.chips * self.rows - self.mats * 128
        if pad:
            self.out[pl.ds(self.mats * 128, pad)] = jnp.zeros((pad, 128), jnp.float32)
        self.give[...] = self.out[self.half(1 - self.core)].astype(jnp.bfloat16)
        self.swap().start()

    def start(self):
        self.swap().wait()
        total = self.out[self.half(self.core)] + self.take[...].astype(jnp.float32)
        self.send[...] = total.astype(jnp.bfloat16)
        for o in range(1, self.chips):
            self.scatter(o).start()

    def middle(self):
        total = self.send[self.slot(self.me)].astype(jnp.float32)
        for o in range(1, self.chips):
            self.scatter(o).wait()
            total = total + self.got[self.slot(self.behind(o))].astype(jnp.float32)
        self.deep[self.slot(self.z)] = total.astype(jnp.bfloat16)
        for o in range(1, self.nz):
            self.along(o).start()

    def last(self):
        for o in range(1, self.nz):
            self.along(o).wait()
        total = self.deep[pl.ds(0, self.rows)].astype(jnp.float32)
        for q in range(1, self.nz):
            total = total + self.deep[pl.ds(q * self.rows, self.rows)].astype(jnp.float32)
        mine = self.slot(self.core * self.chips + self.me)
        self.full[mine] = total.astype(jnp.bfloat16)
        for o in range(1, self.chips):
            self.gather(o).start()
        self.forward(0).start()

    def finish(self):
        for o in range(1, self.chips):
            self.gather(o).wait()
            self.forward(o).start()
        for o in range(self.chips):
            self.forward(o).wait()


def greet(dims):
    nb, nz, nh = dims
    b, z, h = (lax.axis_index(a) for a in AXES)
    me = b * nh + h
    barrier = pltpu.get_barrier_semaphore()
    for o in range(1, nb * nh):
        p = lax.rem(me + o, nb * nh)
        pl.semaphore_signal(
            barrier, inc=1, device_id=(p // nh, z, lax.rem(p, nh)), device_id_type=MESH
        )
    for o in range(1, nz):
        pl.semaphore_signal(
            barrier, inc=1, device_id=(b, lax.rem(z + o, nz), h), device_id_type=MESH
        )
    pl.semaphore_wait(barrier, nb * nh - 1 + nz - 1)


class Edge:
    def __init__(self, src, dst, sems, axis, step):
        size, at = lax.axis_size(axis), lax.axis_index(axis)
        self.sends = at < size - 1 if step > 0 else at > 0
        self.gets = at > 0 if step > 0 else at < size - 1
        self.copy = pltpu.make_async_remote_copy(
            src_ref=src,
            dst_ref=dst,
            send_sem=sems.at[0],
            recv_sem=sems.at[1],
            device_id=tuple(lax.axis_index(a) + (step if a == axis else 0) for a in AXES),
            device_id_type=MESH,
        )
        self.dst = dst

    def start(self):
        @pl.when(self.sends)
        def _():
            self.copy.start()

        @pl.when(jnp.logical_not(self.gets))
        def _():
            self.dst[...] = jnp.zeros(self.dst.shape, self.dst.dtype)

    def arrive(self):
        @pl.when(self.gets)
        def _():
            self.copy.wait_recv()

    def leave(self):
        @pl.when(self.sends)
        def _():
            self.copy.wait_send()


def dot(a, b):
    return jnp.dot(a, b, preferred_element_type=jnp.float32)


def from_left(v, col):
    return jnp.where(col == 0, 0.0, pltpu.roll(v, 1, 0))


def from_right(v, col, width):
    return jnp.where(col == width - 1, 0.0, pltpu.roll(v, v.shape[0] - 1, 0))


def kernel(
    dims, step, x_hbm, ws_hbm, wt_hbm, wd_hbm, c_hbm,
    down_ref, gx_ref, os_ref, ot_ref, od_ref,
    xp, xt, gp, gcat, act, slope, gres, gb, cm, cp, lcat, ct, part, d_out, e_out, d_in, e_in,
    ws_ref, wt_ref, wd_ref, c_ref, wf, wb, tcat, tflip, dflip, dback, load_sems, edge_sems, *sums,
):
    _, rows, width, ch = x_hbm.shape[1:]
    cuts = rows // step
    tokens = rows * width
    per = step * width
    half = len(sums) // 2
    big, small = Sum(dims, 9, sums[:half]), Sum(dims, 6, sums[half:])
    edges = [
        Edge(x_hbm.at[0, :, rows - 1], xp.at[:, 0], edge_sems.at[0], "height", 1),
        Edge(x_hbm.at[0, :, 0], xp.at[:, rows + 1], edge_sems.at[1], "height", -1),
        Edge(gp.at[:, rows], gp.at[:, 0], edge_sems.at[2], "height", 1),
        Edge(gp.at[:, 1], gp.at[:, rows + 1], edge_sems.at[3], "height", -1),
        Edge(d_out, d_in, edge_sems.at[4], "tm", 1),
        Edge(e_out, e_in, edge_sems.at[5], "tm", -1),
    ]
    near = []
    for i in range(cuts):
        at = pl.ds(i * step, step)
        near.append(
            (
                Edge(c_hbm.at[0, 0, at], cm.at[at], edge_sems.at[6 + 2 * i], "tm", 1),
                Edge(c_hbm.at[0, 0, at], cp.at[at], edge_sems.at[7 + 2 * i], "tm", -1),
            )
        )
    loads = [
        pltpu.make_async_copy(src, dst, load_sems.at[i])
        for i, (src, dst) in enumerate(
            (
                (ws_hbm, ws_ref),
                (x_hbm.at[0], xp.at[:, pl.ds(1, rows)]),
                (wt_hbm, wt_ref),
                (wd_hbm, wd_ref),
                (c_hbm, c_ref),
            )
        )
    ]
    inner = (lax.axis_index("tm") > 0).astype(jnp.float32)
    col = lax.broadcasted_iota(jnp.int32, (step, width, ch), 1).reshape(per, ch)

    for copy in loads:
        copy.start()
    greet(dims)
    for e in edges[:2]:
        e.start()
    for pair in near:
        for e in pair:
            e.start()
    for copy in loads:
        copy.wait()
    for dy in range(3):
        for dx in range(3):
            wf[dy * ch : (dy + 1) * ch, dx * ch : (dx + 1) * ch] = ws_ref[dy, dx]

    def flat(v):
        return v.reshape(per, ch)

    def tall(v):
        return v.reshape(step, width, ch)

    def conv(ref, f, starts, count, weights):
        def tap(dy):
            pieces = [ref[f, pl.ds(y + dy, count)].reshape(count * width, ch) for y in starts]
            return jnp.concatenate(pieces, axis=0)

        out = dot(jnp.concatenate([tap(dy) for dy in range(3)], axis=1), weights[...])
        return (
            out[:, ch : 2 * ch]
            + from_left(out[:, :ch], col)
            + from_right(out[:, 2 * ch :], col, width)
        )

    def spread(ref, f, starts, count, v):
        for n, y in enumerate(starts):
            piece = v[n * count * width : (n + 1) * count * width]
            ref[f, pl.ds(y, count)] = piece.reshape(count, width, ch)

    inside = [((y,), step) for y in range(2, rows - 2, step)]
    border = ((0, rows - 2), 2)

    def forward(f, starts, count):
        pre = conv(xp, f, starts, count, wf)
        sig = jax.nn.sigmoid(pre)
        spread(act, f, starts, count, (pre * sig).astype(jnp.bfloat16))
        spread(slope, f, starts, count, sig * (1.0 + pre * (1.0 - sig)))

    for f in range(2):
        for cut in inside:
            forward(f, *cut)
    for f in range(2):
        xt[f, :, width : (rows + 1) * width] = xp[f, pl.ds(1, rows)].reshape(tokens, ch).T
    for k in range(3):
        tcat[:, (2 - k) * ch : (3 - k) * ch] = wt_ref[k]
        tflip[k * ch : (k + 1) * ch, :] = wt_ref[k].T
        dflip[:, k * ch : (k + 1) * ch] = wd_ref[k].T
    dback[0:ch, :] = dflip[:, 2 * ch : 3 * ch]
    dback[ch : 2 * ch, :] = dflip[:, 0:ch]

    for e in edges[:2]:
        e.arrive()
    for f in range(2):
        forward(f, *border)
    for f in range(2):
        xt[f, :, :width] = xp[f, 0].T
        xt[f, :, (rows + 1) * width :] = xp[f, rows + 1].T

    def mixing(i, carry):
        at = pl.ds(i * step, step)
        y0 = dot(flat(act[0, at]), tcat[...])
        y1 = dot(flat(act[1, at]), tcat[...])
        x0 = flat(xp[0, pl.ds(i * step + 1, step)]).astype(jnp.float32)
        x1 = flat(xp[1, pl.ds(i * step + 1, step)]).astype(jnp.float32)
        l0 = (y0[:, :ch] * inner).astype(jnp.bfloat16)
        l1 = (x0 + y0[:, ch : 2 * ch] + y1[:, :ch]).astype(jnp.bfloat16)
        l2 = (x1 + y0[:, 2 * ch :] + y1[:, ch : 2 * ch]).astype(jnp.bfloat16)
        u = y1[:, 2 * ch :].astype(jnp.bfloat16)
        for n, v in enumerate((l0, l1, l2, u)):
            lcat[n, at] = tall(v)
        own = jnp.concatenate([l0, l1, l2], axis=1)
        part[at] = tall(dot(own, wd_ref[...].reshape(3 * ch, ch)))
        ahead = jnp.concatenate([l2, u], axis=1)
        d_out[at] = tall(dot(ahead, wd_ref[0:2].reshape(2 * ch, ch)).astype(jnp.bfloat16))
        e_out[at] = tall(dot(l0, wd_ref[2]).astype(jnp.bfloat16))
        return carry

    lax.fori_loop(0, cuts, mixing, 0)
    for e in edges[4:]:
        e.start()

    ct[ch : 2 * ch, :] = c_ref[0, 0].reshape(tokens, ch).T

    def backward(i):
        at = pl.ds(i * step, step)
        c0, before, after = flat(c_ref[0, 0, at]), flat(cm[at]), flat(cp[at])
        g0 = dot(jnp.concatenate([before, c0], axis=1), dback[...]) * inner
        mid = dot(c0, dflip[:, ch:])
        far = dot(after, dflip[:, : 2 * ch])
        g1, g2, g3 = mid[:, :ch], mid[:, ch:] + far[:, :ch], far[:, ch:]
        gres[0, at] = tall(g1)
        gres[1, at] = tall(g2)
        g = [v.astype(jnp.bfloat16) for v in (g0, g1, g2, g3)]
        for n in range(4):
            gb[n, at] = tall(g[n])
        for a in range(2):
            wide = jnp.concatenate([g[a + 2], g[a + 1], g[a]], axis=1)
            gpre = dot(wide, tflip[...]) * flat(slope[a, at])
            low = gpre.astype(jnp.bfloat16)
            gp[a, pl.ds(i * step + 1, step)] = tall(low)
            gcat[a, at, :, :ch] = tall(from_right(gpre, col, width).astype(jnp.bfloat16))
            gcat[a, at, :, ch : 2 * ch] = tall(low)
            gcat[a, at, :, 2 * ch :] = tall(from_left(gpre, col).astype(jnp.bfloat16))

    for i in range(cuts):
        for e in near[i]:
            e.arrive()
        backward(i)
    for e in edges[2:4]:
        e.start()

    total = jnp.zeros((3 * ch, 3 * ch), jnp.float32)
    for f in range(2):
        left = jnp.concatenate(
            [xt[f, :, dy * width : dy * width + tokens] for dy in range(3)], axis=0
        )
        total = total + dot(left, gcat[f].reshape(tokens, 3 * ch))
    for dy in range(3):
        for dx in range(3):
            big.out[pl.ds((dy * 3 + dx) * ch, ch)] = total[
                dy * ch : (dy + 1) * ch, dx * ch : (dx + 1) * ch
            ]
    big.pair()

    times = jnp.zeros((ch, 3 * ch), jnp.float32)
    for a in range(2):
        wide = jnp.concatenate([gb[n].reshape(tokens, ch) for n in (a + 2, a + 1, a)], axis=1)
        times = times + dot(act[a].reshape(tokens, ch).T, wide)
    big.start()
    ct[0:ch, :] = cp[...].reshape(tokens, ch).T
    ct[2 * ch :, :] = cm[...].reshape(tokens, ch).T
    wide = jnp.concatenate([lcat[n].reshape(tokens, ch) for n in range(4)], axis=1)
    outer = dot(ct[...], wide)

    def block(n, m):
        return outer[m * ch : (m + 1) * ch, n * ch : (n + 1) * ch]

    downs = (block(2, 0) + block(0, 1), block(1, 1) + block(3, 0), block(2, 1) + block(0, 2))
    for k in range(3):
        small.out[pl.ds(k * ch, ch)] = times[:, k * ch : (k + 1) * ch]
        small.out[pl.ds((3 + k) * ch, ch)] = downs[k].T
    small.pair()
    for dy in range(3):
        for dx in range(3):
            at = slice((2 - dy) * ch, (3 - dy) * ch), slice((2 - dx) * ch, (3 - dx) * ch)
            wb[at] = ws_ref[dy, dx].T
    for e in edges[2:4]:
        e.arrive()

    def features(f):
        for starts, count in inside + [border]:
            own = [gres[f, pl.ds(y, count)].reshape(count * width, ch) for y in starts]
            out = conv(gp, f, starts, count, wb) + jnp.concatenate(own, axis=0)
            spread(gx_ref.at[0], f, starts, count, out.astype(jnp.bfloat16))

    features(0)
    small.start()
    big.middle()
    features(1)
    small.middle()
    big.last()
    for e in edges[4:]:
        e.arrive()
    down_ref[0, 0] = (
        part[...] + d_in[...].astype(jnp.float32) + e_in[...].astype(jnp.float32)
    ).astype(jnp.bfloat16)
    small.last()
    big.finish()
    for i in range(9):
        os_ref[i // 3, i % 3] = big.full[pl.ds(i * ch, ch)].astype(jnp.float32)
    small.finish()
    for i in range(3):
        ot_ref[i] = small.full[pl.ds(i * ch, ch)].astype(jnp.float32)
        od_ref[i] = small.full[pl.ds((3 + i) * ch, ch)].astype(jnp.float32)
    for e in edges:
        e.leave()
    for pair in near:
        for e in pair:
            e.leave()


def store(*refs):
    sems = refs[-1]
    copies = [pltpu.make_async_copy(refs[i], refs[5 + i], sems.at[i]) for i in range(5)]
    for copy in copies:
        copy.start()
    for copy in copies:
        copy.wait()


def per_device(features, w_spatial, w_temporal, w_down, cotangent):
    args = (features, w_spatial, w_temporal, w_down, cotangent)
    dims = tuple(lax.axis_size(a) for a in AXES)
    _, frames, rows, width, ch = features.shape
    peers = dims[0] * dims[2]
    step = 4
    bf, f32 = jnp.bfloat16, jnp.float32
    frame = (rows, width, ch)
    shapes = [
        jax.ShapeDtypeStruct(cotangent.shape, bf),
        jax.ShapeDtypeStruct(features.shape, bf),
        jax.ShapeDtypeStruct(w_spatial.shape, f32),
        jax.ShapeDtypeStruct(w_temporal.shape, f32),
        jax.ShapeDtypeStruct(w_down.shape, f32),
    ]
    outs = pl.pallas_call(
        functools.partial(kernel, dims, step),
        out_shape=shapes,
        in_specs=[pl.BlockSpec(memory_space=pltpu.HBM)] * 5,
        out_specs=[pl.BlockSpec(memory_space=pltpu.VMEM)] * 5,
        scratch_shapes=[
            pltpu.VMEM((2, rows + 2, width, ch), bf),
            pltpu.VMEM((2, ch, (rows + 2) * width), bf),
            pltpu.VMEM((2, rows + 2, width, ch), bf),
            pltpu.VMEM((2, rows, width, 3 * ch), bf),
            pltpu.VMEM((2,) + frame, bf),
            pltpu.VMEM((2,) + frame, f32),
            pltpu.VMEM((2,) + frame, f32),
            pltpu.VMEM((4,) + frame, bf),
            pltpu.VMEM(frame, bf),
            pltpu.VMEM(frame, bf),
            pltpu.VMEM((4,) + frame, bf),
            pltpu.VMEM((3 * ch, rows * width), bf),
            pltpu.VMEM(frame, f32),
            pltpu.VMEM(frame, bf),
            pltpu.VMEM(frame, bf),
            pltpu.VMEM(frame, bf),
            pltpu.VMEM(frame, bf),
            pltpu.VMEM(w_spatial.shape, bf),
            pltpu.VMEM(w_temporal.shape, bf),
            pltpu.VMEM(w_down.shape, bf),
            pltpu.VMEM(cotangent.shape, bf),
            pltpu.VMEM((3 * ch, 3 * ch), bf),
            pltpu.VMEM((3 * ch, 3 * ch), bf),
            pltpu.VMEM((ch, 3 * ch), bf),
            pltpu.VMEM((3 * ch, ch), bf),
            pltpu.VMEM((ch, 3 * ch), bf),
            pltpu.VMEM((2 * ch, ch), bf),
            pltpu.SemaphoreType.DMA((5,)),
            pltpu.SemaphoreType.DMA((6 + 2 * rows // step, 2)),
        ]
        + sum_scratch(9, peers, dims[1])
        + sum_scratch(6, peers, dims[1]),
        compiler_params=pltpu.CompilerParams(
            collective_id=0, has_side_effects=True, vmem_limit_bytes=40 * 1024 * 1024
        ),
    )(*(pltpu.with_memory_space_constraint(v, pltpu.HBM) for v in args))
    return pl.pallas_call(
        store,
        out_shape=shapes,
        in_specs=[pl.BlockSpec(memory_space=pltpu.VMEM)] * 5,
        out_specs=[pl.BlockSpec(memory_space=pltpu.HBM)] * 5,
        scratch_shapes=[pltpu.SemaphoreType.DMA((5,))],
        compiler_params=pltpu.CompilerParams(vmem_limit_bytes=4 * 1024 * 1024),
    )(*outs)


def solution(mesh):
    placed = (
        P("batch", "tm", "height", None, None),
        P(),
        P(),
        P(),
        P("batch", "tm", "height", None, None),
    )
    return jax.shard_map(
        per_device,
        mesh=mesh,
        in_specs=placed,
        out_specs=(
            P("batch", "tm", "height", None, None),
            P("batch", "tm", "height", None, None),
            P(),
            P(),
            P(),
        ),
        check_vma=False,
    )
```

```python
import functools

import jax
import jax.numpy as jnp
from jax import lax
from jax.experimental import pallas as pl
from jax.experimental.pallas import tpu as pltpu
from jax.sharding import PartitionSpec as P

MESH = pl.DeviceIdType.MESH
AXES = ("batch", "tm", "height")


def rows_each(mats, peers):
    return 16 * pl.cdiv(mats * 128, 16 * peers)


def sum_scratch(mats, peers, depth):
    rows = rows_each(mats, peers)
    half = peers // 2 * rows
    return [
        pltpu.VMEM((2 * half, 128), jnp.float32),
        pltpu.VMEM((half, 128), jnp.bfloat16),
        pltpu.VMEM((half, 128), jnp.bfloat16),
        pltpu.VMEM((half, 128), jnp.bfloat16),
        pltpu.VMEM((half, 128), jnp.bfloat16),
        pltpu.VMEM((depth * rows, 128), jnp.bfloat16),
        pltpu.VMEM((2 * half, 128), jnp.bfloat16),
        pltpu.SemaphoreType.DMA((5, 2, max(peers // 2, depth))),
    ]


class Sum:
    def __init__(self, dims, mats, refs):
        self.nb, self.nz, self.nh = dims
        self.mats = mats
        self.rows = rows_each(mats, self.nb * self.nh)
        self.out, self.give, self.take, self.send, self.got, self.deep, self.full, self.sems = refs
        self.b, self.z, self.h = (lax.axis_index(a) for a in AXES)
        self.wide = self.nh // 2
        self.chips = self.nb * self.wide
        self.core = lax.rem(self.h, 2)
        self.me = self.b * self.wide + self.h // 2

    def slot(self, i):
        return pl.ds(pl.multiple_of(i * self.rows, 16), self.rows)

    def half(self, core):
        size = self.chips * self.rows
        return pl.ds(pl.multiple_of(core * size, 16), size)

    def copy(self, src, dst, stage, n, dev):
        return pltpu.make_async_remote_copy(
            src_ref=src,
            dst_ref=dst,
            send_sem=self.sems.at[stage, 0, n],
            recv_sem=self.sems.at[stage, 1, n],
            device_id=dev,
            device_id_type=MESH,
        )

    def partner(self):
        return (self.b, self.z, self.h + 1 - 2 * self.core)

    def chip(self, o):
        p = lax.rem(self.me + o, self.chips)
        return p, (p // self.wide, self.z, lax.rem(p, self.wide) * 2 + self.core)

    def behind(self, o):
        return lax.rem(self.me - o + self.chips, self.chips)

    def swap(self):
        return self.copy(self.give, self.take, 0, 0, self.partner())

    def scatter(self, o):
        p, dev = self.chip(o)
        return self.copy(self.send.at[self.slot(p)], self.got.at[self.slot(self.me)], 1, o, dev)

    def along(self, o):
        q = lax.rem(self.z + o, self.nz)
        mine = self.deep.at[self.slot(self.z)]
        return self.copy(mine, mine, 2, o, (self.b, q, self.h))

    def gather(self, o):
        _, dev = self.chip(o)
        mine = self.full.at[self.slot(self.core * self.chips + self.me)]
        return self.copy(mine, mine, 3, o, dev)

    def forward(self, o):
        piece = self.full.at[self.slot(self.core * self.chips + self.behind(o))]
        return self.copy(piece, piece, 4, o, self.partner())

    def pair(self):
        pad = 2 * self.chips * self.rows - self.mats * 128
        if pad:
            self.out[pl.ds(self.mats * 128, pad)] = jnp.zeros((pad, 128), jnp.float32)
        self.give[...] = self.out[self.half(1 - self.core)].astype(jnp.bfloat16)
        self.swap().start()

    def start(self):
        self.swap().wait()
        total = self.out[self.half(self.core)] + self.take[...].astype(jnp.float32)
        self.send[...] = total.astype(jnp.bfloat16)
        for o in range(1, self.chips):
            self.scatter(o).start()

    def middle(self):
        total = self.send[self.slot(self.me)].astype(jnp.float32)
        for o in range(1, self.chips):
            self.scatter(o).wait()
            total = total + self.got[self.slot(self.behind(o))].astype(jnp.float32)
        self.deep[self.slot(self.z)] = total.astype(jnp.bfloat16)
        for o in range(1, self.nz):
            self.along(o).start()

    def last(self):
        for o in range(1, self.nz):
            self.along(o).wait()
        total = self.deep[pl.ds(0, self.rows)].astype(jnp.float32)
        for q in range(1, self.nz):
            total = total + self.deep[pl.ds(q * self.rows, self.rows)].astype(jnp.float32)
        mine = self.slot(self.core * self.chips + self.me)
        self.full[mine] = total.astype(jnp.bfloat16)
        for o in range(1, self.chips):
            self.gather(o).start()
        self.forward(0).start()

    def relay(self):
        for o in range(1, self.chips):
            self.gather(o).wait()
            self.forward(o).start()

    def finish(self):
        for o in range(self.chips):
            self.forward(o).wait()


def greet(dims):
    nb, nz, nh = dims
    b, z, h = (lax.axis_index(a) for a in AXES)
    me = b * nh + h
    barrier = pltpu.get_barrier_semaphore()
    for o in range(1, nb * nh):
        p = lax.rem(me + o, nb * nh)
        pl.semaphore_signal(
            barrier, inc=1, device_id=(p // nh, z, lax.rem(p, nh)), device_id_type=MESH
        )
    for o in range(1, nz):
        pl.semaphore_signal(
            barrier, inc=1, device_id=(b, lax.rem(z + o, nz), h), device_id_type=MESH
        )
    pl.semaphore_wait(barrier, nb * nh - 1 + nz - 1)


class Edge:
    def __init__(self, src, dst, sems, axis, step):
        size, at = lax.axis_size(axis), lax.axis_index(axis)
        self.sends = at < size - 1 if step > 0 else at > 0
        self.gets = at > 0 if step > 0 else at < size - 1
        self.copy = pltpu.make_async_remote_copy(
            src_ref=src,
            dst_ref=dst,
            send_sem=sems.at[0],
            recv_sem=sems.at[1],
            device_id=tuple(lax.axis_index(a) + (step if a == axis else 0) for a in AXES),
            device_id_type=MESH,
        )
        self.dst = dst

    def start(self):
        @pl.when(self.sends)
        def _():
            self.copy.start()

        @pl.when(jnp.logical_not(self.gets))
        def _():
            self.dst[...] = jnp.zeros(self.dst.shape, self.dst.dtype)

    def arrive(self):
        @pl.when(self.gets)
        def _():
            self.copy.wait_recv()

    def leave(self):
        @pl.when(self.sends)
        def _():
            self.copy.wait_send()


def dot(a, b):
    return jnp.dot(a, b, preferred_element_type=jnp.float32)


def from_left(v, col):
    return jnp.where(col == 0, 0.0, pltpu.roll(v, 1, 0))


def from_right(v, col, width):
    return jnp.where(col == width - 1, 0.0, pltpu.roll(v, v.shape[0] - 1, 0))


def kernel(
    dims, step, x_hbm, ws_hbm, wt_hbm, wd_hbm, c_hbm,
    down_ref, gx_ref, os_ref, ot_ref, od_ref,
    xp, xt, gp, gcat, act, slope, gres, gb, cm, cp, lcat, ct, part, d_out, e_out, d_in, e_in,
    ws_ref, wt_ref, wd_ref, c_ref, wf, wb, tcat, tflip, dflip, dback, load_sems, edge_sems, *sums,
):
    _, rows, width, ch = x_hbm.shape[1:]
    cuts = rows // step
    tokens = rows * width
    per = step * width
    half = len(sums) // 2
    big, small = Sum(dims, 9, sums[:half]), Sum(dims, 6, sums[half:])
    edges = [
        Edge(x_hbm.at[0, :, rows - 1], xp.at[:, 0], edge_sems.at[0], "height", 1),
        Edge(x_hbm.at[0, :, 0], xp.at[:, rows + 1], edge_sems.at[1], "height", -1),
        Edge(gp.at[:, rows], gp.at[:, 0], edge_sems.at[2], "height", 1),
        Edge(gp.at[:, 1], gp.at[:, rows + 1], edge_sems.at[3], "height", -1),
        Edge(d_out, d_in, edge_sems.at[4], "tm", 1),
        Edge(e_out, e_in, edge_sems.at[5], "tm", -1),
    ]
    near = []
    for i in range(cuts):
        at = pl.ds(i * step, step)
        near.append(
            (
                Edge(c_hbm.at[0, 0, at], cm.at[at], edge_sems.at[6 + 2 * i], "tm", 1),
                Edge(c_hbm.at[0, 0, at], cp.at[at], edge_sems.at[7 + 2 * i], "tm", -1),
            )
        )
    loads = [
        pltpu.make_async_copy(src, dst, load_sems.at[i])
        for i, (src, dst) in enumerate(
            (
                (ws_hbm, ws_ref),
                (x_hbm.at[0], xp.at[:, pl.ds(1, rows)]),
                (wt_hbm, wt_ref),
                (wd_hbm, wd_ref),
                (c_hbm, c_ref),
            )
        )
    ]
    inner = (lax.axis_index("tm") > 0).astype(jnp.float32)
    col = lax.broadcasted_iota(jnp.int32, (step, width, ch), 1).reshape(per, ch)

    for copy in loads:
        copy.start()
    greet(dims)
    for e in edges[:2]:
        e.start()
    for pair in near:
        for e in pair:
            e.start()
    for copy in loads:
        copy.wait()
    for dy in range(3):
        for dx in range(3):
            wf[dy * ch : (dy + 1) * ch, dx * ch : (dx + 1) * ch] = ws_ref[dy, dx]

    def flat(v):
        return v.reshape(per, ch)

    def tall(v):
        return v.reshape(step, width, ch)

    def conv(ref, f, starts, count, weights):
        def tap(dy):
            pieces = [ref[f, pl.ds(y + dy, count)].reshape(count * width, ch) for y in starts]
            return jnp.concatenate(pieces, axis=0)

        out = dot(jnp.concatenate([tap(dy) for dy in range(3)], axis=1), weights[...])
        return (
            out[:, ch : 2 * ch]
            + from_left(out[:, :ch], col)
            + from_right(out[:, 2 * ch :], col, width)
        )

    def spread(ref, f, starts, count, v):
        for n, y in enumerate(starts):
            piece = v[n * count * width : (n + 1) * count * width]
            ref[f, pl.ds(y, count)] = piece.reshape(count, width, ch)

    inside = [((y,), step) for y in range(2, rows - 2, step)]
    border = ((0, rows - 2), 2)

    def forward(f, starts, count):
        pre = conv(xp, f, starts, count, wf)
        sig = jax.nn.sigmoid(pre)
        spread(act, f, starts, count, (pre * sig).astype(jnp.bfloat16))
        spread(slope, f, starts, count, sig * (1.0 + pre * (1.0 - sig)))

    for f in range(2):
        for cut in inside:
            forward(f, *cut)
    for f in range(2):
        xt[f, :, width : (rows + 1) * width] = xp[f, pl.ds(1, rows)].reshape(tokens, ch).T
    for k in range(3):
        tcat[:, (2 - k) * ch : (3 - k) * ch] = wt_ref[k]
        tflip[k * ch : (k + 1) * ch, :] = wt_ref[k].T
        dflip[:, k * ch : (k + 1) * ch] = wd_ref[k].T
    dback[0:ch, :] = dflip[:, 2 * ch : 3 * ch]
    dback[ch : 2 * ch, :] = dflip[:, 0:ch]

    for e in edges[:2]:
        e.arrive()
    for f in range(2):
        forward(f, *border)
    for f in range(2):
        xt[f, :, :width] = xp[f, 0].T
        xt[f, :, (rows + 1) * width :] = xp[f, rows + 1].T

    def mixing(i, carry):
        at = pl.ds(i * step, step)
        y0 = dot(flat(act[0, at]), tcat[...])
        y1 = dot(flat(act[1, at]), tcat[...])
        x0 = flat(xp[0, pl.ds(i * step + 1, step)]).astype(jnp.float32)
        x1 = flat(xp[1, pl.ds(i * step + 1, step)]).astype(jnp.float32)
        l0 = (y0[:, :ch] * inner).astype(jnp.bfloat16)
        l1 = (x0 + y0[:, ch : 2 * ch] + y1[:, :ch]).astype(jnp.bfloat16)
        l2 = (x1 + y0[:, 2 * ch :] + y1[:, ch : 2 * ch]).astype(jnp.bfloat16)
        u = y1[:, 2 * ch :].astype(jnp.bfloat16)
        for n, v in enumerate((l0, l1, l2, u)):
            lcat[n, at] = tall(v)
        own = jnp.concatenate([l0, l1, l2], axis=1)
        part[at] = tall(dot(own, wd_ref[...].reshape(3 * ch, ch)))
        ahead = jnp.concatenate([l2, u], axis=1)
        d_out[at] = tall(dot(ahead, wd_ref[0:2].reshape(2 * ch, ch)).astype(jnp.bfloat16))
        e_out[at] = tall(dot(l0, wd_ref[2]).astype(jnp.bfloat16))
        return carry

    lax.fori_loop(0, cuts, mixing, 0)

    ct[ch : 2 * ch, :] = c_ref[0, 0].reshape(tokens, ch).T

    def backward(i):
        at = pl.ds(i * step, step)
        c0, before, after = flat(c_ref[0, 0, at]), flat(cm[at]), flat(cp[at])
        g0 = dot(jnp.concatenate([before, c0], axis=1), dback[...]) * inner
        mid = dot(c0, dflip[:, ch:])
        far = dot(after, dflip[:, : 2 * ch])
        g1, g2, g3 = mid[:, :ch], mid[:, ch:] + far[:, :ch], far[:, ch:]
        gres[0, at] = tall(g1)
        gres[1, at] = tall(g2)
        g = [v.astype(jnp.bfloat16) for v in (g0, g1, g2, g3)]
        for n in range(4):
            gb[n, at] = tall(g[n])
        for a in range(2):
            wide = jnp.concatenate([g[a + 2], g[a + 1], g[a]], axis=1)
            gpre = dot(wide, tflip[...]) * flat(slope[a, at])
            low = gpre.astype(jnp.bfloat16)
            gp[a, pl.ds(i * step + 1, step)] = tall(low)
            gcat[a, at, :, :ch] = tall(from_right(gpre, col, width).astype(jnp.bfloat16))
            gcat[a, at, :, ch : 2 * ch] = tall(low)
            gcat[a, at, :, 2 * ch :] = tall(from_left(gpre, col).astype(jnp.bfloat16))

    for i in range(cuts):
        for e in near[i]:
            e.arrive()
        if i == cuts - 1:
            for e in edges[4:]:
                e.start()
        backward(i)
    for e in edges[2:4]:
        e.start()

    total = jnp.zeros((3 * ch, 3 * ch), jnp.float32)
    for f in range(2):
        left = jnp.concatenate(
            [xt[f, :, dy * width : dy * width + tokens] for dy in range(3)], axis=0
        )
        total = total + dot(left, gcat[f].reshape(tokens, 3 * ch))
    for dy in range(3):
        for dx in range(3):
            big.out[pl.ds((dy * 3 + dx) * ch, ch)] = total[
                dy * ch : (dy + 1) * ch, dx * ch : (dx + 1) * ch
            ]
    big.pair()

    times = jnp.zeros((ch, 3 * ch), jnp.float32)
    for a in range(2):
        wide = jnp.concatenate([gb[n].reshape(tokens, ch) for n in (a + 2, a + 1, a)], axis=1)
        times = times + dot(act[a].reshape(tokens, ch).T, wide)
    big.start()
    ct[0:ch, :] = cp[...].reshape(tokens, ch).T
    ct[2 * ch :, :] = cm[...].reshape(tokens, ch).T
    wide = jnp.concatenate([lcat[n].reshape(tokens, ch) for n in range(4)], axis=1)
    outer = dot(ct[...], wide)

    def block(n, m):
        return outer[m * ch : (m + 1) * ch, n * ch : (n + 1) * ch]

    downs = (block(2, 0) + block(0, 1), block(1, 1) + block(3, 0), block(2, 1) + block(0, 2))
    for k in range(3):
        small.out[pl.ds(k * ch, ch)] = times[:, k * ch : (k + 1) * ch]
        small.out[pl.ds((3 + k) * ch, ch)] = downs[k].T
    small.pair()
    for dy in range(3):
        for dx in range(3):
            at = slice((2 - dy) * ch, (3 - dy) * ch), slice((2 - dx) * ch, (3 - dx) * ch)
            wb[at] = ws_ref[dy, dx].T
    for e in edges[2:4]:
        e.arrive()

    def features(f):
        for starts, count in inside + [border]:
            own = [gres[f, pl.ds(y, count)].reshape(count * width, ch) for y in starts]
            out = conv(gp, f, starts, count, wb) + jnp.concatenate(own, axis=0)
            spread(gx_ref.at[0], f, starts, count, out.astype(jnp.bfloat16))

    features(0)
    small.start()
    big.middle()
    features(1)
    small.middle()
    big.last()
    for e in edges[4:]:
        e.arrive()
    down_ref[0, 0] = (
        part[...] + d_in[...].astype(jnp.float32) + e_in[...].astype(jnp.float32)
    ).astype(jnp.bfloat16)
    small.last()
    big.relay()
    big.finish()
    for i in range(9):
        os_ref[i // 3, i % 3] = big.full[pl.ds(i * ch, ch)].astype(jnp.float32)
    small.relay()
    small.finish()
    for i in range(3):
        ot_ref[i] = small.full[pl.ds(i * ch, ch)].astype(jnp.float32)
        od_ref[i] = small.full[pl.ds((3 + i) * ch, ch)].astype(jnp.float32)
    for e in edges:
        e.leave()
    for pair in near:
        for e in pair:
            e.leave()


def store(*refs):
    sems = refs[-1]
    copies = [pltpu.make_async_copy(refs[i], refs[5 + i], sems.at[i]) for i in range(5)]
    for copy in copies:
        copy.start()
    for copy in copies:
        copy.wait()


def per_device(features, w_spatial, w_temporal, w_down, cotangent):
    args = (features, w_spatial, w_temporal, w_down, cotangent)
    dims = tuple(lax.axis_size(a) for a in AXES)
    _, frames, rows, width, ch = features.shape
    peers = dims[0] * dims[2]
    step = 4
    bf, f32 = jnp.bfloat16, jnp.float32
    frame = (rows, width, ch)
    shapes = [
        jax.ShapeDtypeStruct(cotangent.shape, bf),
        jax.ShapeDtypeStruct(features.shape, bf),
        jax.ShapeDtypeStruct(w_spatial.shape, f32),
        jax.ShapeDtypeStruct(w_temporal.shape, f32),
        jax.ShapeDtypeStruct(w_down.shape, f32),
    ]
    outs = pl.pallas_call(
        functools.partial(kernel, dims, step),
        out_shape=shapes,
        in_specs=[pl.BlockSpec(memory_space=pltpu.HBM)] * 5,
        out_specs=[pl.BlockSpec(memory_space=pltpu.VMEM)] * 5,
        scratch_shapes=[
            pltpu.VMEM((2, rows + 2, width, ch), bf),
            pltpu.VMEM((2, ch, (rows + 2) * width), bf),
            pltpu.VMEM((2, rows + 2, width, ch), bf),
            pltpu.VMEM((2, rows, width, 3 * ch), bf),
            pltpu.VMEM((2,) + frame, bf),
            pltpu.VMEM((2,) + frame, f32),
            pltpu.VMEM((2,) + frame, f32),
            pltpu.VMEM((4,) + frame, bf),
            pltpu.VMEM(frame, bf),
            pltpu.VMEM(frame, bf),
            pltpu.VMEM((4,) + frame, bf),
            pltpu.VMEM((3 * ch, rows * width), bf),
            pltpu.VMEM(frame, f32),
            pltpu.VMEM(frame, bf),
            pltpu.VMEM(frame, bf),
            pltpu.VMEM(frame, bf),
            pltpu.VMEM(frame, bf),
            pltpu.VMEM(w_spatial.shape, bf),
            pltpu.VMEM(w_temporal.shape, bf),
            pltpu.VMEM(w_down.shape, bf),
            pltpu.VMEM(cotangent.shape, bf),
            pltpu.VMEM((3 * ch, 3 * ch), bf),
            pltpu.VMEM((3 * ch, 3 * ch), bf),
            pltpu.VMEM((ch, 3 * ch), bf),
            pltpu.VMEM((3 * ch, ch), bf),
            pltpu.VMEM((ch, 3 * ch), bf),
            pltpu.VMEM((2 * ch, ch), bf),
            pltpu.SemaphoreType.DMA((5,)),
            pltpu.SemaphoreType.DMA((6 + 2 * rows // step, 2)),
        ]
        + sum_scratch(9, peers, dims[1])
        + sum_scratch(6, peers, dims[1]),
        compiler_params=pltpu.CompilerParams(
            collective_id=0, has_side_effects=True, vmem_limit_bytes=40 * 1024 * 1024
        ),
    )(*(pltpu.with_memory_space_constraint(v, pltpu.HBM) for v in args))
    return pl.pallas_call(
        store,
        out_shape=shapes,
        in_specs=[pl.BlockSpec(memory_space=pltpu.VMEM)] * 5,
        out_specs=[pl.BlockSpec(memory_space=pltpu.HBM)] * 5,
        scratch_shapes=[pltpu.SemaphoreType.DMA((5,))],
        compiler_params=pltpu.CompilerParams(vmem_limit_bytes=4 * 1024 * 1024),
    )(*outs)


def solution(mesh):
    placed = (
        P("batch", "tm", "height", None, None),
        P(),
        P(),
        P(),
        P("batch", "tm", "height", None, None),
    )
    return jax.shard_map(
        per_device,
        mesh=mesh,
        in_specs=placed,
        out_specs=(
            P("batch", "tm", "height", None, None),
            P("batch", "tm", "height", None, None),
            P(),
            P(),
            P(),
        ),
        check_vma=False,
    )
```

```python
import functools

import jax
import jax.numpy as jnp
from jax import lax
from jax.experimental import pallas as pl
from jax.experimental.pallas import tpu as pltpu
from jax.sharding import PartitionSpec as P

MESH = pl.DeviceIdType.MESH
AXES = ("batch", "tm", "height")


def rows_each(mats, peers):
    return 16 * pl.cdiv(mats * 128, 16 * peers)


def sum_scratch(mats, peers, depth):
    rows = rows_each(mats, peers)
    half = peers // 2 * rows
    return [
        pltpu.VMEM((2 * half, 128), jnp.float32),
        pltpu.VMEM((half, 128), jnp.bfloat16),
        pltpu.VMEM((half, 128), jnp.bfloat16),
        pltpu.VMEM((half, 128), jnp.bfloat16),
        pltpu.VMEM((half, 128), jnp.bfloat16),
        pltpu.VMEM((depth * rows, 128), jnp.bfloat16),
        pltpu.VMEM((2 * half, 128), jnp.bfloat16),
        pltpu.SemaphoreType.DMA((5, 2, max(peers // 2, depth))),
    ]


class Sum:
    def __init__(self, dims, mats, refs):
        self.nb, self.nz, self.nh = dims
        self.mats = mats
        self.rows = rows_each(mats, self.nb * self.nh)
        self.out, self.give, self.take, self.send, self.got, self.deep, self.full, self.sems = refs
        self.b, self.z, self.h = (lax.axis_index(a) for a in AXES)
        self.wide = self.nh // 2
        self.chips = self.nb * self.wide
        self.core = lax.rem(self.h, 2)
        self.me = self.b * self.wide + self.h // 2

    def slot(self, i):
        return pl.ds(pl.multiple_of(i * self.rows, 16), self.rows)

    def half(self, core):
        size = self.chips * self.rows
        return pl.ds(pl.multiple_of(core * size, 16), size)

    def copy(self, src, dst, stage, n, dev):
        return pltpu.make_async_remote_copy(
            src_ref=src,
            dst_ref=dst,
            send_sem=self.sems.at[stage, 0, n],
            recv_sem=self.sems.at[stage, 1, n],
            device_id=dev,
            device_id_type=MESH,
        )

    def partner(self):
        return (self.b, self.z, self.h + 1 - 2 * self.core)

    def chip(self, o):
        p = lax.rem(self.me + o, self.chips)
        return p, (p // self.wide, self.z, lax.rem(p, self.wide) * 2 + self.core)

    def behind(self, o):
        return lax.rem(self.me - o + self.chips, self.chips)

    def swap(self):
        return self.copy(self.give, self.take, 0, 0, self.partner())

    def scatter(self, o):
        p, dev = self.chip(o)
        return self.copy(self.send.at[self.slot(p)], self.got.at[self.slot(self.me)], 1, o, dev)

    def along(self, o):
        q = lax.rem(self.z + o, self.nz)
        mine = self.deep.at[self.slot(self.z)]
        return self.copy(mine, mine, 2, o, (self.b, q, self.h))

    def gather(self, o):
        _, dev = self.chip(o)
        mine = self.full.at[self.slot(self.core * self.chips + self.me)]
        return self.copy(mine, mine, 3, o, dev)

    def forward(self, o):
        piece = self.full.at[self.slot(self.core * self.chips + self.behind(o))]
        return self.copy(piece, piece, 4, o, self.partner())

    def pair(self):
        pad = 2 * self.chips * self.rows - self.mats * 128
        if pad:
            self.out[pl.ds(self.mats * 128, pad)] = jnp.zeros((pad, 128), jnp.float32)
        self.give[...] = self.out[self.half(1 - self.core)].astype(jnp.bfloat16)
        self.swap().start()

    def start(self):
        self.swap().wait()
        total = self.out[self.half(self.core)] + self.take[...].astype(jnp.float32)
        self.send[...] = total.astype(jnp.bfloat16)
        for o in range(1, self.chips):
            self.scatter(o).start()

    def middle(self):
        total = self.send[self.slot(self.me)].astype(jnp.float32)
        for o in range(1, self.chips):
            self.scatter(o).wait()
            total = total + self.got[self.slot(self.behind(o))].astype(jnp.float32)
        self.deep[self.slot(self.z)] = total.astype(jnp.bfloat16)
        for o in range(1, self.nz):
            self.along(o).start()

    def last(self):
        for o in range(1, self.nz):
            self.along(o).wait()
        total = self.deep[pl.ds(0, self.rows)].astype(jnp.float32)
        for q in range(1, self.nz):
            total = total + self.deep[pl.ds(q * self.rows, self.rows)].astype(jnp.float32)
        mine = self.slot(self.core * self.chips + self.me)
        self.full[mine] = total.astype(jnp.bfloat16)
        for o in range(1, self.chips):
            self.gather(o).start()
        self.forward(0).start()

    def relay(self):
        for o in range(1, self.chips):
            self.gather(o).wait()
            self.forward(o).start()

    def finish(self):
        for o in range(self.chips):
            self.forward(o).wait()


def greet(dims):
    nb, nz, nh = dims
    b, z, h = (lax.axis_index(a) for a in AXES)
    me = b * nh + h
    barrier = pltpu.get_barrier_semaphore()
    for o in range(1, nb * nh):
        p = lax.rem(me + o, nb * nh)
        pl.semaphore_signal(
            barrier, inc=1, device_id=(p // nh, z, lax.rem(p, nh)), device_id_type=MESH
        )
    for o in range(1, nz):
        pl.semaphore_signal(
            barrier, inc=1, device_id=(b, lax.rem(z + o, nz), h), device_id_type=MESH
        )
    pl.semaphore_wait(barrier, nb * nh - 1 + nz - 1)


class Edge:
    def __init__(self, src, dst, sems, axis, step):
        size, at = lax.axis_size(axis), lax.axis_index(axis)
        self.sends = at < size - 1 if step > 0 else at > 0
        self.gets = at > 0 if step > 0 else at < size - 1
        self.copy = pltpu.make_async_remote_copy(
            src_ref=src,
            dst_ref=dst,
            send_sem=sems.at[0],
            recv_sem=sems.at[1],
            device_id=tuple(lax.axis_index(a) + (step if a == axis else 0) for a in AXES),
            device_id_type=MESH,
        )
        self.dst = dst

    def start(self):
        @pl.when(self.sends)
        def _():
            self.copy.start()

        @pl.when(jnp.logical_not(self.gets))
        def _():
            self.dst[...] = jnp.zeros(self.dst.shape, self.dst.dtype)

    def arrive(self):
        @pl.when(self.gets)
        def _():
            self.copy.wait_recv()

    def leave(self):
        @pl.when(self.sends)
        def _():
            self.copy.wait_send()


def dot(a, b):
    return jnp.dot(a, b, preferred_element_type=jnp.float32)


def from_left(v, col):
    return jnp.where(col == 0, 0.0, pltpu.roll(v, 1, 0))


def from_right(v, col, width):
    return jnp.where(col == width - 1, 0.0, pltpu.roll(v, v.shape[0] - 1, 0))


def kernel(
    dims, step, x_hbm, ws_hbm, wt_hbm, wd_hbm, c_hbm,
    down_ref, gx_ref, os_ref, ot_ref, od_ref,
    xp, xt, gp, gcat, act, slope, gres, gb, cm, cp, lcat, ct, part, d_out, e_out, d_in, e_in,
    ws_ref, wt_ref, wd_ref, c_ref, wf, wb, tcat, tflip, dflip, dback, load_sems, edge_sems, *sums,
):
    _, rows, width, ch = x_hbm.shape[1:]
    cuts = rows // step
    tokens = rows * width
    per = step * width
    half = len(sums) // 2
    big, small = Sum(dims, 9, sums[:half]), Sum(dims, 6, sums[half:])
    edges = [
        Edge(x_hbm.at[0, :, rows - 1], xp.at[:, 0], edge_sems.at[0], "height", 1),
        Edge(x_hbm.at[0, :, 0], xp.at[:, rows + 1], edge_sems.at[1], "height", -1),
        Edge(gp.at[:, rows], gp.at[:, 0], edge_sems.at[2], "height", 1),
        Edge(gp.at[:, 1], gp.at[:, rows + 1], edge_sems.at[3], "height", -1),
        Edge(d_out, d_in, edge_sems.at[4], "tm", 1),
        Edge(e_out, e_in, edge_sems.at[5], "tm", -1),
    ]
    near = []
    for i in range(cuts):
        at = pl.ds(i * step, step)
        near.append(
            (
                Edge(c_hbm.at[0, 0, at], cm.at[at], edge_sems.at[6 + 2 * i], "tm", 1),
                Edge(c_hbm.at[0, 0, at], cp.at[at], edge_sems.at[7 + 2 * i], "tm", -1),
            )
        )
    loads = [
        pltpu.make_async_copy(src, dst, load_sems.at[i])
        for i, (src, dst) in enumerate(
            (
                (ws_hbm, ws_ref),
                (x_hbm.at[0], xp.at[:, pl.ds(1, rows)]),
                (wt_hbm, wt_ref),
                (wd_hbm, wd_ref),
                (c_hbm, c_ref),
            )
        )
    ]
    inner = (lax.axis_index("tm") > 0).astype(jnp.float32)
    col = lax.broadcasted_iota(jnp.int32, (step, width, ch), 1).reshape(per, ch)

    for copy in loads:
        copy.start()
    greet(dims)
    for e in edges[:2]:
        e.start()
    for pair in near:
        for e in pair:
            e.start()
    for copy in loads:
        copy.wait()
    for dy in range(3):
        for dx in range(3):
            wf[dy * ch : (dy + 1) * ch, dx * ch : (dx + 1) * ch] = ws_ref[dy, dx]

    def flat(v):
        return v.reshape(per, ch)

    def tall(v):
        return v.reshape(step, width, ch)

    def conv(ref, f, starts, count, weights):
        def tap(dy):
            pieces = [ref[f, pl.ds(y + dy, count)].reshape(count * width, ch) for y in starts]
            return jnp.concatenate(pieces, axis=0)

        out = dot(jnp.concatenate([tap(dy) for dy in range(3)], axis=1), weights[...])
        return (
            out[:, ch : 2 * ch]
            + from_left(out[:, :ch], col)
            + from_right(out[:, 2 * ch :], col, width)
        )

    def spread(ref, f, starts, count, v):
        for n, y in enumerate(starts):
            piece = v[n * count * width : (n + 1) * count * width]
            ref[f, pl.ds(y, count)] = piece.reshape(count, width, ch)

    inside = [((y,), step) for y in range(2, rows - 2, step)]
    border = ((0, rows - 2), 2)

    def forward(f, starts, count):
        pre = conv(xp, f, starts, count, wf)
        sig = jax.nn.sigmoid(pre)
        spread(act, f, starts, count, (pre * sig).astype(jnp.bfloat16))
        spread(slope, f, starts, count, sig * (1.0 + pre * (1.0 - sig)))

    for f in range(2):
        for cut in inside:
            forward(f, *cut)
    for f in range(2):
        xt[f, :, width : (rows + 1) * width] = xp[f, pl.ds(1, rows)].reshape(tokens, ch).T
    for k in range(3):
        tcat[:, (2 - k) * ch : (3 - k) * ch] = wt_ref[k]
        tflip[k * ch : (k + 1) * ch, :] = wt_ref[k].T
        dflip[:, k * ch : (k + 1) * ch] = wd_ref[k].T
    dback[0:ch, :] = dflip[:, 2 * ch : 3 * ch]
    dback[ch : 2 * ch, :] = dflip[:, 0:ch]

    for e in edges[:2]:
        e.arrive()
    for f in range(2):
        forward(f, *border)
    for f in range(2):
        xt[f, :, :width] = xp[f, 0].T
        xt[f, :, (rows + 1) * width :] = xp[f, rows + 1].T

    def mixing(i, carry):
        at = pl.ds(i * step, step)
        y0 = dot(flat(act[0, at]), tcat[...])
        y1 = dot(flat(act[1, at]), tcat[...])
        x0 = flat(xp[0, pl.ds(i * step + 1, step)]).astype(jnp.float32)
        x1 = flat(xp[1, pl.ds(i * step + 1, step)]).astype(jnp.float32)
        l0 = (y0[:, :ch] * inner).astype(jnp.bfloat16)
        l1 = (x0 + y0[:, ch : 2 * ch] + y1[:, :ch]).astype(jnp.bfloat16)
        l2 = (x1 + y0[:, 2 * ch :] + y1[:, ch : 2 * ch]).astype(jnp.bfloat16)
        u = y1[:, 2 * ch :].astype(jnp.bfloat16)
        for n, v in enumerate((l0, l1, l2, u)):
            lcat[n, at] = tall(v)
        own = jnp.concatenate([l0, l1, l2], axis=1)
        part[at] = tall(dot(own, wd_ref[...].reshape(3 * ch, ch)))
        ahead = jnp.concatenate([l2, u], axis=1)
        d_out[at] = tall(dot(ahead, wd_ref[0:2].reshape(2 * ch, ch)).astype(jnp.bfloat16))
        e_out[at] = tall(dot(l0, wd_ref[2]).astype(jnp.bfloat16))
        return carry

    lax.fori_loop(0, cuts, mixing, 0)

    ct[ch : 2 * ch, :] = c_ref[0, 0].reshape(tokens, ch).T

    def backward(i):
        at = pl.ds(i * step, step)
        c0, before, after = flat(c_ref[0, 0, at]), flat(cm[at]), flat(cp[at])
        g0 = dot(jnp.concatenate([before, c0], axis=1), dback[...]) * inner
        mid = dot(c0, dflip[:, ch:])
        far = dot(after, dflip[:, : 2 * ch])
        g1, g2, g3 = mid[:, :ch], mid[:, ch:] + far[:, :ch], far[:, ch:]
        gres[0, at] = tall(g1)
        gres[1, at] = tall(g2)
        g = [v.astype(jnp.bfloat16) for v in (g0, g1, g2, g3)]
        for n in range(4):
            gb[n, at] = tall(g[n])
        for a in range(2):
            wide = jnp.concatenate([g[a + 2], g[a + 1], g[a]], axis=1)
            gpre = dot(wide, tflip[...]) * flat(slope[a, at])
            low = gpre.astype(jnp.bfloat16)
            gp[a, pl.ds(i * step + 1, step)] = tall(low)
            gcat[a, at, :, :ch] = tall(from_right(gpre, col, width).astype(jnp.bfloat16))
            gcat[a, at, :, ch : 2 * ch] = tall(low)
            gcat[a, at, :, 2 * ch :] = tall(from_left(gpre, col).astype(jnp.bfloat16))

    for i in range(cuts):
        for e in near[i]:
            e.arrive()
        if i == cuts - 1:
            for e in edges[4:]:
                e.start()
        backward(i)
    for e in edges[2:4]:
        e.start()

    total = jnp.zeros((3 * ch, 3 * ch), jnp.float32)
    for f in range(2):
        left = jnp.concatenate(
            [xt[f, :, dy * width : dy * width + tokens] for dy in range(3)], axis=0
        )
        total = total + dot(left, gcat[f].reshape(tokens, 3 * ch))
    for dy in range(3):
        for dx in range(3):
            big.out[pl.ds((dy * 3 + dx) * ch, ch)] = total[
                dy * ch : (dy + 1) * ch, dx * ch : (dx + 1) * ch
            ]
    big.pair()

    times = jnp.zeros((ch, 3 * ch), jnp.float32)
    for a in range(2):
        wide = jnp.concatenate([gb[n].reshape(tokens, ch) for n in (a + 2, a + 1, a)], axis=1)
        times = times + dot(act[a].reshape(tokens, ch).T, wide)
        if a == 0:
            big.start()
    ct[0:ch, :] = cp[...].reshape(tokens, ch).T
    ct[2 * ch :, :] = cm[...].reshape(tokens, ch).T
    wide = jnp.concatenate([lcat[n].reshape(tokens, ch) for n in range(4)], axis=1)
    outer = dot(ct[...], wide)

    def block(n, m):
        return outer[m * ch : (m + 1) * ch, n * ch : (n + 1) * ch]

    downs = (block(2, 0) + block(0, 1), block(1, 1) + block(3, 0), block(2, 1) + block(0, 2))
    for k in range(3):
        small.out[pl.ds(k * ch, ch)] = times[:, k * ch : (k + 1) * ch]
        small.out[pl.ds((3 + k) * ch, ch)] = downs[k].T
    small.pair()
    big.middle()
    for dy in range(3):
        for dx in range(3):
            at = slice((2 - dy) * ch, (3 - dy) * ch), slice((2 - dx) * ch, (3 - dx) * ch)
            wb[at] = ws_ref[dy, dx].T
    for e in edges[2:4]:
        e.arrive()

    def features(f):
        for starts, count in inside + [border]:
            own = [gres[f, pl.ds(y, count)].reshape(count * width, ch) for y in starts]
            out = conv(gp, f, starts, count, wb) + jnp.concatenate(own, axis=0)
            spread(gx_ref.at[0], f, starts, count, out.astype(jnp.bfloat16))

    features(0)
    small.start()
    features(1)
    small.middle()
    big.last()
    for e in edges[4:]:
        e.arrive()
    down_ref[0, 0] = (
        part[...] + d_in[...].astype(jnp.float32) + e_in[...].astype(jnp.float32)
    ).astype(jnp.bfloat16)
    small.last()
    big.relay()
    big.finish()
    for i in range(9):
        os_ref[i // 3, i % 3] = big.full[pl.ds(i * ch, ch)].astype(jnp.float32)
    small.relay()
    small.finish()
    for i in range(3):
        ot_ref[i] = small.full[pl.ds(i * ch, ch)].astype(jnp.float32)
        od_ref[i] = small.full[pl.ds((3 + i) * ch, ch)].astype(jnp.float32)
    for e in edges:
        e.leave()
    for pair in near:
        for e in pair:
            e.leave()


def store(*refs):
    sems = refs[-1]
    copies = [pltpu.make_async_copy(refs[i], refs[5 + i], sems.at[i]) for i in range(5)]
    for copy in copies:
        copy.start()
    for copy in copies:
        copy.wait()


def per_device(features, w_spatial, w_temporal, w_down, cotangent):
    args = (features, w_spatial, w_temporal, w_down, cotangent)
    dims = tuple(lax.axis_size(a) for a in AXES)
    _, frames, rows, width, ch = features.shape
    peers = dims[0] * dims[2]
    step = 4
    bf, f32 = jnp.bfloat16, jnp.float32
    frame = (rows, width, ch)
    shapes = [
        jax.ShapeDtypeStruct(cotangent.shape, bf),
        jax.ShapeDtypeStruct(features.shape, bf),
        jax.ShapeDtypeStruct(w_spatial.shape, f32),
        jax.ShapeDtypeStruct(w_temporal.shape, f32),
        jax.ShapeDtypeStruct(w_down.shape, f32),
    ]
    outs = pl.pallas_call(
        functools.partial(kernel, dims, step),
        out_shape=shapes,
        in_specs=[pl.BlockSpec(memory_space=pltpu.HBM)] * 5,
        out_specs=[pl.BlockSpec(memory_space=pltpu.VMEM)] * 5,
        scratch_shapes=[
            pltpu.VMEM((2, rows + 2, width, ch), bf),
            pltpu.VMEM((2, ch, (rows + 2) * width), bf),
            pltpu.VMEM((2, rows + 2, width, ch), bf),
            pltpu.VMEM((2, rows, width, 3 * ch), bf),
            pltpu.VMEM((2,) + frame, bf),
            pltpu.VMEM((2,) + frame, f32),
            pltpu.VMEM((2,) + frame, f32),
            pltpu.VMEM((4,) + frame, bf),
            pltpu.VMEM(frame, bf),
            pltpu.VMEM(frame, bf),
            pltpu.VMEM((4,) + frame, bf),
            pltpu.VMEM((3 * ch, rows * width), bf),
            pltpu.VMEM(frame, f32),
            pltpu.VMEM(frame, bf),
            pltpu.VMEM(frame, bf),
            pltpu.VMEM(frame, bf),
            pltpu.VMEM(frame, bf),
            pltpu.VMEM(w_spatial.shape, bf),
            pltpu.VMEM(w_temporal.shape, bf),
            pltpu.VMEM(w_down.shape, bf),
            pltpu.VMEM(cotangent.shape, bf),
            pltpu.VMEM((3 * ch, 3 * ch), bf),
            pltpu.VMEM((3 * ch, 3 * ch), bf),
            pltpu.VMEM((ch, 3 * ch), bf),
            pltpu.VMEM((3 * ch, ch), bf),
            pltpu.VMEM((ch, 3 * ch), bf),
            pltpu.VMEM((2 * ch, ch), bf),
            pltpu.SemaphoreType.DMA((5,)),
            pltpu.SemaphoreType.DMA((6 + 2 * rows // step, 2)),
        ]
        + sum_scratch(9, peers, dims[1])
        + sum_scratch(6, peers, dims[1]),
        compiler_params=pltpu.CompilerParams(
            collective_id=0, has_side_effects=True, vmem_limit_bytes=40 * 1024 * 1024
        ),
    )(*(pltpu.with_memory_space_constraint(v, pltpu.HBM) for v in args))
    return pl.pallas_call(
        store,
        out_shape=shapes,
        in_specs=[pl.BlockSpec(memory_space=pltpu.VMEM)] * 5,
        out_specs=[pl.BlockSpec(memory_space=pltpu.HBM)] * 5,
        scratch_shapes=[pltpu.SemaphoreType.DMA((5,))],
        compiler_params=pltpu.CompilerParams(vmem_limit_bytes=4 * 1024 * 1024),
    )(*outs)


def solution(mesh):
    placed = (
        P("batch", "tm", "height", None, None),
        P(),
        P(),
        P(),
        P("batch", "tm", "height", None, None),
    )
    return jax.shard_map(
        per_device,
        mesh=mesh,
        in_specs=placed,
        out_specs=(
            P("batch", "tm", "height", None, None),
            P("batch", "tm", "height", None, None),
            P(),
            P(),
            P(),
        ),
        check_vma=False,
    )
```
